32 devices in a mesh: groups: 2 (over y), lon: 4 (over z), lat: 4 (over x, core).
Axes of the slice: x: 2, y: 2, z: 4, core: 2. Of those that a mesh axis runs over, the one named last changes fastest.
Arguments:
- fields: bfloat16 [768, 112, 256], P(('groups', 'lat'), 'lon'), parts along dimension 0, may hold values from -6 to 6
- norm_gains: float32 [3, 256], replicated, may hold values from 0.25 to 1.75
- lon_qkv: bfloat16 [256, 768], replicated, may hold values from -0.375 to 0.375
- lon_out: bfloat16 [256, 256], replicated, may hold values from -0.375 to 0.375
- lat_qkv: bfloat16 [256, 768], replicated, may hold values from -0.375 to 0.375
- lat_out: bfloat16 [256, 256], replicated, may hold values from -0.375 to 0.375
- logit_scales: float32 [2, 8], replicated, may hold values from 0.08 to 7.6
- conv_taps: float32 [25, 256], replicated, may hold values from -1.25 to 1.25
- mlp_in: bfloat16 [256, 2048], replicated, may hold values from -0.375 to 0.375
- mlp_down: bfloat16 [1024, 256], replicated, may hold values from -0.1875 to 0.1875
Outputs:
- mixed_grid: bfloat16 [768, 112, 256], P(('groups', 'lat'), 'lon'), parts along dimension 0
The draws below stay inside these ranges and needn't reach their ends.
There are 2 independent parts, one for each index of `groups`. The reference program is written for one: setup_inputs(seed, part) draws one part's arguments, and reference() takes and returns one part's arrays. A program takes and returns all parts, laid end to end along the dimension named above; an argument that names none is the same for every part. Nothing has to cross between parts.
All inputs are finite; a program needn't handle non-finite values.
Results may differ from the reference program's by a relative error of at most 0.019.
The reference program's roundings to bfloat16 on the way count: a program that leaves them out, or rounds other values in their place, can miss the bound.
Values may be sent and summed in bfloat16 or wider, within the bound.
A program may use at most 64 MiB of HBM per device.

```python
import math
import jax
import jax.numpy as jnp
from jax import lax

D = 256
HEADS = 8
HD = 32
HID = 1024
KERNEL = 5
NLAT = 384
NLON = 112


def draw_logit_scales(key, part):
    factor = jnp.exp(jax.random.uniform(key, (2, HEADS), jnp.float32, math.log(0.5), math.log(2.0)))
    return (factor * HD ** (-0.5)).astype(jnp.float32)


def level_of(rng, extent, cuts, low, top_value):
    factor_of, own = 1.0, jax.random.fold_in(rng, 6)
    for position, parts in cuts:
        draws = jnp.exp(jax.random.uniform(jax.random.fold_in(own, position), (parts,), jnp.float32, low / len(cuts), top_value / len(cuts)))
        factor_of = factor_of * jnp.repeat(draws, extent[position] // parts).reshape([-1 if axis == position else 1 for axis in range(len(extent))])
    return factor_of


def bell_draw(key, dims, scale, bound, cuts=(), kind=jnp.bfloat16):
    array = scale * jax.random.normal(key, dims, jnp.float32)
    if cuts:
        array = array * level_of(key, dims, cuts, -0.22, 0.18)
    return jnp.clip(array, -bound, bound).astype(kind)


def setup_inputs(seed: int = 0, part: int = 0) -> dict:
    keys = jax.random.split(jax.random.key(seed), 11)
    part_keys = jax.random.split(jax.random.fold_in(keys[10], part), 11)
    return {
        "fields": bell_draw(part_keys[0], (NLAT, NLON, D), 1.0, 6.0, ((0, 4), (1, 4))),
        "norm_gains": jnp.clip(1.0 + 0.15 * jax.random.normal(keys[1], (3, D), jnp.float32), 0.25, 1.75),
        "lon_qkv": bell_draw(keys[2], (D, 3 * D), D ** -0.5, 0.375),
        "lon_out": bell_draw(keys[3], (D, D), D ** -0.5, 0.375),
        "lat_qkv": bell_draw(keys[4], (D, 3 * D), D ** -0.5, 0.375),
        "lat_out": bell_draw(keys[5], (D, D), D ** -0.5, 0.375),
        "logit_scales": draw_logit_scales(jax.random.fold_in(keys[10], 71), part),
        "conv_taps": bell_draw(keys[7], (KERNEL * KERNEL, D), (KERNEL * KERNEL) ** -0.5, 1.25, (), jnp.float32),
        "mlp_in": bell_draw(keys[8], (D, 2 * HID), D ** -0.5, 0.375),
        "mlp_down": bell_draw(keys[9], (HID, D), HID ** -0.5, 0.1875),
    }


EPSILON = 1e-05

def layer_norm(values, gains):
    average = lax.optimization_barrier(jnp.mean(values, -1, keepdims=True))
    centred = values - average
    spread = lax.optimization_barrier(jnp.mean(centred * centred, -1, keepdims=True))
    return centred * lax.rsqrt(spread + EPSILON) * gains

def line_attention(one_line, qkv_weight, out_weight, factors):
    features = one_line.shape[-1]
    heads = factors.shape[0]
    qkv_all = jnp.dot(one_line, qkv_weight, preferred_element_type=jnp.float32).astype(jnp.bfloat16)
    qkv_all = lax.optimization_barrier(qkv_all).astype(jnp.float32)
    queries = qkv_all[:, :features].reshape(-1, heads, features // heads)
    keys_in = qkv_all[:, features:2 * features].reshape(-1, heads, features // heads)
    values_in = qkv_all[:, 2 * features:].reshape(-1, heads, features // heads)
    scores = jnp.einsum('qhd,khd->hqk', queries, keys_in) * factors[:, None, None]
    weights = jnp.exp(scores - lax.optimization_barrier(jnp.max(scores, -1, keepdims=True)))
    totals = lax.optimization_barrier(jnp.sum(weights, -1))
    rounded = lax.optimization_barrier(weights.astype(jnp.bfloat16)).astype(jnp.float32)
    context = jnp.einsum('hqk,khd->qhd', rounded, values_in) / jnp.transpose(totals)[:, :, None]
    context = context.reshape(-1, features).astype(jnp.bfloat16)
    return jnp.dot(context, out_weight, preferred_element_type=jnp.float32).astype(jnp.bfloat16)

def reference(fields, norm_gains, lon_qkv, lon_out, lat_qkv, lat_out, logit_scales, conv_taps, mlp_in, mlp_down):
    anchor = fields.astype(jnp.float32)
    normed = layer_norm(anchor, norm_gains[0]).astype(jnp.bfloat16)
    lon_mix = lax.map(lambda one_line: line_attention(one_line, lon_qkv, lon_out, logit_scales[0]), normed)
    first_state = (anchor + lon_mix.astype(jnp.float32)).astype(jnp.bfloat16)
    first_wide = first_state.astype(jnp.float32)
    normed = layer_norm(first_wide, norm_gains[1]).astype(jnp.bfloat16)
    columns = jnp.swapaxes(normed, 0, 1)
    lat_mix = lax.map(lambda one_line: line_attention(one_line, lat_qkv, lat_out, logit_scales[1]), columns)
    lat_mix = jnp.swapaxes(lat_mix, 0, 1)
    second_state = (first_wide + lat_mix.astype(jnp.float32)).astype(jnp.bfloat16)
    grid_wide = second_state.astype(jnp.float32)
    margin = KERNEL // 2
    padded = jnp.pad(grid_wide, ((margin, margin), (0, 0), (0, 0)))
    padded = jnp.concatenate([padded[:, NLON - margin:], padded, padded[:, :margin]], axis=1)
    smoothed = jnp.zeros((NLAT, NLON, D), jnp.float32)
    for row_tap in range(KERNEL):
        for col_tap in range(KERNEL):
            smoothed = smoothed + conv_taps[row_tap * KERNEL + col_tap] * padded[row_tap:row_tap + NLAT, col_tap:col_tap + NLON]
    normed = layer_norm(smoothed, norm_gains[2]).astype(jnp.bfloat16)
    gate_up = jnp.dot(normed.reshape(-1, D), mlp_in, preferred_element_type=jnp.float32)
    hidden = (jax.nn.silu(gate_up[:, :HID]) * gate_up[:, HID:]).astype(jnp.bfloat16)
    update = jnp.dot(hidden, mlp_down, preferred_element_type=jnp.float32).reshape(NLAT, NLON, D)
    return (grid_wide + update).astype(jnp.bfloat16)
```

```python
import functools
import math

import jax
import jax.numpy as jnp
from jax import lax
from jax.experimental import pallas as pl
from jax.experimental.pallas import tpu as pltpu
from jax.sharding import PartitionSpec as P

KERNEL = 5
LANES = 128
EPSILON = 1e-05
MESH = pl.DeviceIdType.MESH
F32, BF16 = jnp.float32, jnp.bfloat16
NT = (((1,), (1,)), ((), ()))
TN = (((0,), (0,)), ((), ()))


def extended(x, sides, width, wrap):
    for axis, dim in sides:
        count, length = (lax.axis_size(axis), x.shape[dim])
        up = [(i, (i + 1) % count) for i in range(count if wrap else count - 1)]
        down = [(j, i) for i, j in up]
        last = lax.slice_in_dim(x, length - width, length, axis=dim)
        leading = lax.slice_in_dim(x, 0, width, axis=dim)
        before = lax.ppermute(last, axis, up)
        after = lax.ppermute(leading, axis, down)
        x = jnp.concatenate([before, x, after], axis=dim)
    return x


def layer_norm(values, gains):
    average = jnp.mean(values, -1, keepdims=True)
    centred = values - average
    spread = jnp.mean(centred * centred, -1, keepdims=True)
    return centred * lax.rsqrt(spread + EPSILON) * gains


def attend(x, wqk, wvt, wout, factor_of, heads, valid):
    features = x.shape[-1]
    size = features // heads
    qk = jnp.dot(x, wqk, preferred_element_type=F32).astype(BF16)
    queries, keys = qk[:, :features], qk[:, features:]
    values = lax.dot_general(wvt, x, NT, preferred_element_type=F32).astype(BF16)
    lane = lax.broadcasted_iota(jnp.int32, (1, features), 1) // size
    parts = []
    for h in range(heads):
        own = keys * (lane == h).astype(F32).astype(BF16)
        scores = lax.dot_general(own, queries, NT, preferred_element_type=F32)
        if valid is not None:
            scores = jnp.where(valid, scores, -1e30)
        top = jnp.max(scores, 0, keepdims=True)
        weights = jnp.exp2((scores - top) * (factor_of(h) * math.log2(math.e)))
        total = jnp.sum(weights, 0, keepdims=True)
        part = jnp.dot(
            values[h * size : (h + 1) * size], weights.astype(BF16), preferred_element_type=F32
        )
        parts.append(part / total)
    context = jnp.concatenate(parts, 0).astype(BF16)
    return lax.dot_general(context, wout, TN, preferred_element_type=F32).astype(BF16)


def attention_kernel(
    n, m, heads, lon_cols, chunk,
    x_ref, gains, wqk1, wvt1, wo1, wqk2, wvt2, wo2, scales,
    out_ref,
    xs, recv, obuf, ret, normed, state, lsend, lrecv, lout, lret,
    fs, fr, bs, br, gs, gr, hs, hr,
):
    rows_own = xs.shape[1]
    width, features = xs.shape[2], xs.shape[3]
    chunks = rows_own // chunk
    band = chunk * n
    lat_rows = rows_own * n
    cols_own = lon_cols // m
    halves = features // LANES
    me = lax.axis_index("lon")
    mine = lax.axis_index("lat")
    lon_peers = [lax.rem(me + d, n) for d in range(1, n)]
    lat_peers = [lax.rem(mine + d, m) for d in range(1, m)]

    barrier = pltpu.get_barrier_semaphore()
    for peer in lon_peers:
        pl.semaphore_signal(barrier, inc=1, device_id={"lon": peer}, device_id_type=MESH)
    for peer in lat_peers:
        pl.semaphore_signal(barrier, inc=1, device_id={"lat": peer}, device_id_type=MESH)
    pl.semaphore_wait(barrier, n + m - 2)

    def forth(ch, d):
        peer = lon_peers[d]
        part = pl.ds(ch * chunk, chunk)
        return pltpu.make_async_remote_copy(
            src_ref=xs.at[peer, part], dst_ref=recv.at[me, part],
            send_sem=fs.at[ch, d], recv_sem=fr.at[ch, d],
            device_id={"lon": peer}, device_id_type=MESH,
        )

    def back(ch, d):
        peer = lon_peers[d]
        part = pl.ds(ch * chunk, chunk)
        return pltpu.make_async_remote_copy(
            src_ref=obuf.at[peer, part], dst_ref=ret.at[me, part],
            send_sem=bs.at[ch, d], recv_sem=br.at[ch, d],
            device_id={"lon": peer}, device_id_type=MESH,
        )

    def lat_forth(ch, d):
        peer = lat_peers[d]
        part = pl.ds(pl.multiple_of(ch * band, band), band)
        return pltpu.make_async_remote_copy(
            src_ref=lsend.at[pl.ds(peer * cols_own, cols_own), part],
            dst_ref=lrecv.at[mine, pl.ds(0, cols_own), part],
            send_sem=gs.at[ch, d], recv_sem=gr.at[ch, d],
            device_id={"lat": peer}, device_id_type=MESH,
        )

    def lat_back(c, d):
        peer = lat_peers[d]
        return pltpu.make_async_remote_copy(
            src_ref=lout.at[peer, c], dst_ref=lret.at[mine * cols_own + c],
            send_sem=hs.at[c, d], recv_sem=hr.at[c, d],
            device_id={"lat": peer}, device_id_type=MESH,
        )

    @pl.loop(0, chunks)
    def _(ch):
        part = pl.ds(ch * chunk, chunk)
        for o in range(n):
            block = x_ref[pl.ds(o * rows_own + ch * chunk, chunk)].astype(F32)
            xs[o, part] = layer_norm(block, gains[0:1][None]).astype(BF16)
        for d in range(n - 1):
            forth(ch, d).start()
        recv[me, part] = xs[me, part]

    position = lax.broadcasted_iota(jnp.int32, (n * width, 1), 0)
    valid = lax.rem(position, width) < lon_cols

    def finish_chunk(ch):
        for d in range(n - 1):
            back(ch, d).wait_recv()
        part = pl.ds(ch * chunk, chunk)
        for o in range(n):
            block = x_ref[pl.ds(o * rows_own + ch * chunk, chunk)].astype(F32)
            first = (block + ret[o, part].astype(F32)).astype(BF16).astype(F32)
            base = o * chunk * width
            start = pl.multiple_of(ch * (band * width) + base, chunk * width)
            first2 = first.reshape(chunk * width, features)
            second_norm = layer_norm(first2, gains[1:2])
            for half in range(halves):
                lanes = slice(half * LANES, (half + 1) * LANES)
                state[half, pl.ds(start, chunk * width), :] = first2[:, lanes]
                normed[half, pl.ds(base, chunk * width), :] = second_norm[:, lanes]
        rows = pl.ds(pl.multiple_of(ch * band, band), band)
        for c in range(lon_cols):
            for half in range(halves):
                lanes = slice(half * LANES, (half + 1) * LANES)
                column = normed.at[half][pl.ds(c, band, stride=width), :]
                lsend[c, rows, lanes] = column.astype(BF16)
        for d in range(m - 1):
            lat_forth(ch, d).start()
        lrecv[mine, :, rows, :] = lsend[pl.ds(mine * cols_own, cols_own), rows, :]

    @pl.loop(0, chunks)
    def _(ch):
        for d in range(n - 1):
            forth(ch, d).wait_recv()

        @pl.loop(0, chunk)
        def _(i):
            row = ch * chunk + i
            line = recv[:, row].reshape(n * width, features)
            mixed = attend(line, wqk1[...], wvt1[...], wo1[...], lambda h: scales[0, h], heads, valid)
            obuf[:, row] = mixed.reshape(n, width, features)

        for d in range(n - 1):
            back(ch, d).start()
        part = pl.ds(ch * chunk, chunk)
        ret[me, part] = obuf[me, part]

        @pl.when(ch > 0)
        def _():
            finish_chunk(ch - 1)

    finish_chunk(chunks - 1)

    @pl.loop(0, chunks)
    def _(ch):
        for d in range(m - 1):
            lat_forth(ch, d).wait_recv()

    @pl.loop(0, cols_own)
    def _(c):
        line = lrecv[:, c].reshape(m * lat_rows, features)
        mixed = attend(line, wqk2[...], wvt2[...], wo2[...], lambda h: scales[1, h], heads, None)
        lout[:, c] = mixed.reshape(m, lat_rows, features)
        for d in range(m - 1):
            lat_back(c, d).start()
        lret[mine * cols_own + c] = lout[mine, c]

    def add_column(col):
        place = pl.ds(col, lat_rows, stride=width)
        for half in range(halves):
            lanes = slice(half * LANES, (half + 1) * LANES)
            total = state.at[half][place, :] + lret[col, :, lanes].astype(F32)
            state.at[half][place, :] = total.astype(BF16).astype(F32)

    @pl.loop(0, cols_own)
    def _(c):
        add_column(mine * cols_own + c)

    @pl.loop(0, cols_own)
    def _(c):
        for d in range(m - 1):
            lat_back(c, d).wait_recv()
            source = lax.rem(mine + m - (d + 1), m)
            add_column(source * cols_own + c)

    @pl.loop(0, chunks)
    def _(ch):
        for o in range(n):
            start = pl.multiple_of(ch * (band * width) + o * chunk * width, chunk * width)
            for half in range(halves):
                lanes = slice(half * LANES, (half + 1) * LANES)
                block = state[half, pl.ds(start, chunk * width), :].astype(BF16)
                out_ref[pl.ds(o * rows_own + ch * chunk, chunk), :, lanes] = block.reshape(
                    chunk, width, LANES
                )
        for d in range(n - 1):
            forth(ch, d).wait_send()
            back(ch, d).wait_send()
        for d in range(m - 1):
            lat_forth(ch, d).wait_send()

    @pl.loop(0, cols_own)
    def _(c):
        for d in range(m - 1):
            lat_back(c, d).wait_send()


def chunk_of(rows_own, n):
    for size in range(4, rows_own + 1):
        if rows_own % size == 0 and (size * n) % 16 == 0:
            return size
    return rows_own


def attention(fields, norm_gains, lon_qkv, lon_out, lat_qkv, lat_out, logit_scales):
    lat_rows, lon_cols, features = fields.shape
    heads = logit_scales.shape[1]
    n, m = lax.axis_size("lon"), lax.axis_size("lat")
    width = -(-lon_cols // 16) * 16
    rows_own, cols_own = lat_rows // n, lon_cols // m
    chunk = chunk_of(rows_own, n)
    chunks, band = rows_own // chunk, chunk * n
    padded = jnp.pad(fields, ((0, 0), (0, width - lon_cols), (0, 0)))
    vmem = pl.BlockSpec(memory_space=pltpu.VMEM)
    dma = pltpu.SemaphoreType.DMA
    split = 2 * features
    return pl.pallas_call(
        functools.partial(attention_kernel, n, m, heads, lon_cols, chunk),
        out_shape=jax.ShapeDtypeStruct((lat_rows, width, features), BF16),
        in_specs=[vmem] * 8 + [pl.BlockSpec(memory_space=pltpu.SMEM)],
        out_specs=vmem,
        scratch_shapes=[
            pltpu.VMEM((n, rows_own, width, features), BF16),
            pltpu.VMEM((n, rows_own, width, features), BF16),
            pltpu.VMEM((n, rows_own, width, features), BF16),
            pltpu.VMEM((n, rows_own, width, features), BF16),
            pltpu.VMEM((features // LANES, band * width, LANES), F32),
            pltpu.VMEM((features // LANES, lat_rows * width, LANES), F32),
            pltpu.VMEM((lon_cols, lat_rows, features), BF16),
            pltpu.VMEM((m, cols_own, lat_rows, features), BF16),
            pltpu.VMEM((m, cols_own, lat_rows, features), BF16),
            pltpu.VMEM((lon_cols, lat_rows, features), BF16),
            dma((chunks, n - 1)), dma((chunks, n - 1)),
            dma((chunks, n - 1)), dma((chunks, n - 1)),
            dma((chunks, m - 1)), dma((chunks, m - 1)),
            dma((cols_own, m - 1)), dma((cols_own, m - 1)),
        ],
        compiler_params=pltpu.CompilerParams(
            collective_id=0, has_side_effects=True, vmem_limit_bytes=60 * 2**20
        ),
    )(
        padded, norm_gains,
        lon_qkv[:, :split], lon_qkv[:, split:].T, lon_out,
        lat_qkv[:, :split], lat_qkv[:, split:].T, lat_out,
        logit_scales,
    )


def mixer_kernel(rows, lon_cols, wide, taps, gains, w_in, w_down, out):
    step = pl.program_id(0)
    width, features = wide.shape[1], wide.shape[2]
    hidden_len = w_down.shape[0]
    margin = KERNEL // 2
    lines = wide[pl.ds(step * rows, rows + 2 * margin)].astype(F32)
    smoothed = None
    for dx in range(KERNEL):
        term = None
        for dy in range(KERNEL):
            tap = taps[pl.ds(dy * KERNEL + dx, 1), :][None]
            piece = tap * lines[dy : dy + rows]
            term = piece if term is None else term + piece
        if dx:
            term = pltpu.roll(term, width - dx, 1)
        smoothed = term if smoothed is None else smoothed + term
    normed = layer_norm(smoothed.reshape(rows * width, features), gains[2:3]).astype(BF16)
    gate_up = jnp.dot(normed, w_in[...], preferred_element_type=F32)
    half = gate_up[:, :hidden_len] * 0.5
    hidden = (half * (1.0 + jnp.tanh(half)) * gate_up[:, hidden_len:]).astype(BF16)
    update = jnp.dot(hidden, w_down[...], preferred_element_type=F32)
    centre = pltpu.roll(lines[margin : margin + rows], width - margin, 1)
    total = centre + update.reshape(rows, width, features)
    out[...] = total[:, :lon_cols].astype(BF16)


def mixer(second, conv_taps, norm_gains, mlp_in, mlp_down):
    lat_rows, lon_cols, features = second.shape
    margin = KERNEL // 2
    widened = extended(second, (("lon", 1),), margin, True)
    widened = extended(widened, (("lat", 0),), margin, False)
    width = -(-widened.shape[1] // 16) * 16
    widened = jnp.pad(widened, ((0, 0), (0, width - widened.shape[1]), (0, 0)))
    rows = next(r for r in (8, 6, 4, 3, 2, 1) if lat_rows % r == 0)
    vmem = pl.BlockSpec(memory_space=pltpu.VMEM)
    return pl.pallas_call(
        functools.partial(mixer_kernel, rows, lon_cols),
        grid=(lat_rows // rows,),
        out_shape=jax.ShapeDtypeStruct((lat_rows, lon_cols, features), BF16),
        in_specs=[vmem] * 5,
        out_specs=pl.BlockSpec((rows, lon_cols, features), lambda i: (i, 0, 0)),
        compiler_params=pltpu.CompilerParams(vmem_limit_bytes=48 * 2**20),
    )(widened, conv_taps, norm_gains, mlp_in, mlp_down)


def per_device(
    fields, norm_gains, lon_qkv, lon_out, lat_qkv, lat_out, logit_scales, conv_taps, mlp_in, mlp_down
):
    lon_cols = fields.shape[1]
    second = attention(fields, norm_gains, lon_qkv, lon_out, lat_qkv, lat_out, logit_scales)
    return mixer(second[:, :lon_cols], conv_taps, norm_gains, mlp_in, mlp_down)


def solution(mesh):
    in_specs = (P(("groups", "lat"), "lon", None), P(), P(), P(), P(), P(), P(), P(), P(), P())
    out_specs = P(("groups", "lat"), "lon", None)
    return jax.shard_map(
        per_device, mesh=mesh, in_specs=in_specs, out_specs=out_specs, check_vma=False
    )
```

```python
import functools
import math

import jax
import jax.numpy as jnp
from jax import lax
from jax.experimental import pallas as pl
from jax.experimental.pallas import tpu as pltpu
from jax.sharding import PartitionSpec as P

KERNEL = 5
LANES = 128
EPSILON = 1e-05
MESH = pl.DeviceIdType.MESH
F32, BF16 = jnp.float32, jnp.bfloat16
NT = (((1,), (1,)), ((), ()))
TN = (((0,), (0,)), ((), ()))


def extended(x, sides, width, wrap):
    for axis, dim in sides:
        count, length = (lax.axis_size(axis), x.shape[dim])
        up = [(i, (i + 1) % count) for i in range(count if wrap else count - 1)]
        down = [(j, i) for i, j in up]
        last = lax.slice_in_dim(x, length - width, length, axis=dim)
        leading = lax.slice_in_dim(x, 0, width, axis=dim)
        before = lax.ppermute(last, axis, up)
        after = lax.ppermute(leading, axis, down)
        x = jnp.concatenate([before, x, after], axis=dim)
    return x


def layer_norm(values, gains):
    average = jnp.mean(values, -1, keepdims=True)
    centred = values - average
    spread = jnp.mean(centred * centred, -1, keepdims=True)
    return centred * lax.rsqrt(spread + EPSILON) * gains


def attend(x, wqk, wvt, wout, factor_of, heads, valid):
    features = x.shape[-1]
    size = features // heads
    qk = jnp.dot(x, wqk, preferred_element_type=F32).astype(BF16)
    queries, keys = qk[:, :features], qk[:, features:]
    values = lax.dot_general(wvt, x, NT, preferred_element_type=F32).astype(BF16)
    lane = lax.broadcasted_iota(jnp.int32, (1, features), 1) // size
    parts = []
    for h in range(heads):
        own = keys * (lane == h).astype(F32).astype(BF16)
        scores = lax.dot_general(own, queries, NT, preferred_element_type=F32)
        if valid is not None:
            scores = jnp.where(valid, scores, -1e30)
        top = jnp.max(scores, 0, keepdims=True)
        weights = jnp.exp2((scores - top) * (factor_of(h) * math.log2(math.e)))
        total = jnp.sum(weights, 0, keepdims=True)
        part = jnp.dot(
            values[h * size : (h + 1) * size], weights.astype(BF16), preferred_element_type=F32
        )
        parts.append(part / total)
    context = jnp.concatenate(parts, 0).astype(BF16)
    return lax.dot_general(context, wout, TN, preferred_element_type=F32)


def attention_kernel(
    n, m, heads, lon_cols, chunk,
    x_ref, gains, wqkv1, wo1, wqkv2, wo2, scales,
    out_ref,
    xs, recv, wide, mixed, obuf, ret, state, lsend, lrecv, lout, lret, wvt1, wvt2,
    fs, fr, bs, br, gs, gr, hs, hr,
):
    rows_own = xs.shape[1]
    width, features = xs.shape[2], xs.shape[3]
    chunks = rows_own // chunk
    lat_rows = rows_own * n
    cols_own = lon_cols // m
    halves = features // LANES
    split = 2 * features
    segment = obuf.shape[2]
    me = lax.axis_index("lon")
    mine = lax.axis_index("lat")
    lon_peers = [lax.rem(me + d, n) for d in range(1, n)]
    lat_peers = [lax.rem(mine + d, m) for d in range(1, m)]

    barrier = pltpu.get_barrier_semaphore()
    for peer in lon_peers:
        pl.semaphore_signal(barrier, inc=1, device_id={"lon": peer}, device_id_type=MESH)
    for peer in lat_peers:
        pl.semaphore_signal(barrier, inc=1, device_id={"lat": peer}, device_id_type=MESH)
    pl.semaphore_wait(barrier, n + m - 2)

    def forth(ch, d):
        peer = lon_peers[d]
        part = pl.ds(ch * chunk, chunk)
        return pltpu.make_async_remote_copy(
            src_ref=xs.at[peer, part], dst_ref=recv.at[me, part],
            send_sem=fs.at[ch, d], recv_sem=fr.at[ch, d],
            device_id={"lon": peer}, device_id_type=MESH,
        )

    def back(c, d):
        peer = lon_peers[d]
        return pltpu.make_async_remote_copy(
            src_ref=obuf.at[peer, c], dst_ref=ret.at[me, c],
            send_sem=bs.at[c, d], recv_sem=br.at[c, d],
            device_id={"lon": peer}, device_id_type=MESH,
        )

    def lat_forth(c, d):
        peer = lat_peers[d]
        return pltpu.make_async_remote_copy(
            src_ref=lsend.at[peer, c], dst_ref=lrecv.at[mine, c],
            send_sem=gs.at[c, d], recv_sem=gr.at[c, d],
            device_id={"lat": peer}, device_id_type=MESH,
        )

    def lat_back(c, d):
        peer = lat_peers[d]
        return pltpu.make_async_remote_copy(
            src_ref=lout.at[peer, c], dst_ref=lret.at[mine, c],
            send_sem=hs.at[c, d], recv_sem=hr.at[c, d],
            device_id={"lat": peer}, device_id_type=MESH,
        )

    @pl.loop(0, chunks)
    def _(ch):
        part = pl.ds(ch * chunk, chunk)
        for o in range(n):
            first_row = o * rows_own + ch * chunk
            block = x_ref[pl.ds(first_row, chunk)].astype(F32)
            xs[o, part] = layer_norm(block, gains[0:1][None]).astype(BF16)
        for d in range(n - 1):
            forth(ch, d).start()
        recv[me, part] = xs[me, part]

    wvt1[...] = wqkv1[:, split:].astype(F32).T.astype(BF16)
    wvt2[...] = wqkv2[:, split:].astype(F32).T.astype(BF16)

    @pl.loop(0, lat_rows // chunk)
    def _(i):
        block = x_ref[pl.ds(i * chunk, chunk)].astype(F32).reshape(chunk * width, features)
        place = pl.ds(pl.multiple_of(i * (chunk * width), chunk * width), chunk * width)
        for half in range(halves):
            wide[half, place, :] = block[:, half * LANES : (half + 1) * LANES]

    @pl.loop(0, cols_own)
    def _(c):
        for p in range(m):
            for half in range(halves):
                place = pl.ds(p * cols_own + c, lat_rows, stride=width)
                state[c, p, :, half * LANES : (half + 1) * LANES] = wide.at[half][place, :]

    position = lax.broadcasted_iota(jnp.int32, (n * width, 1), 0)
    valid = lax.rem(position, width) < lon_cols

    @pl.loop(0, chunks)
    def _(ch):
        for d in range(n - 1):
            forth(ch, d).wait_recv()

        @pl.loop(0, chunk)
        def _(i):
            row = ch * chunk + i
            line = recv[:, row].reshape(n * width, features)
            result = attend(
                line, wqkv1[:, :split], wvt1[...], wo1[...], lambda h: scales[0, h], heads, valid
            )
            place = pl.ds(row, n * width, stride=rows_own)
            for half in range(halves):
                mixed.at[half][place, :] = result[:, half * LANES : (half + 1) * LANES]

    spare = segment - m * rows_own

    @pl.loop(0, cols_own)
    def _(c):
        for j in range(n):
            for half in range(halves):
                pieces = []
                for p in range(m):
                    start = (j * width + p * cols_own + c) * rows_own
                    if rows_own % 8 == 0:
                        start = pl.multiple_of(start, 8)
                    pieces.append(mixed[half, pl.ds(start, rows_own), :])
                if spare:
                    pieces.append(jnp.zeros((spare, LANES), F32))
                block = jnp.concatenate(pieces, 0).astype(BF16)
                obuf[j, c, :, half * LANES : (half + 1) * LANES] = block
        for d in range(n - 1):
            back(c, d).start()
        ret[me, c] = obuf[me, c]

    def finish_lon(c):
        for d in range(n - 1):
            back(c, d).wait_recv()
        arrived = [ret[o, c].astype(F32) for o in range(n)]
        for p in range(m):
            lon_mix = jnp.concatenate(
                [block[p * rows_own : (p + 1) * rows_own] for block in arrived], 0
            )
            first = (state[c, p] + lon_mix).astype(BF16).astype(F32)
            state[c, p] = first
            lsend[p, c] = layer_norm(first, gains[1:2]).astype(BF16)
        for d in range(m - 1):
            lat_forth(c, d).start()
        lrecv[mine, c] = lsend[mine, c]

    def lat_line(c):
        for d in range(m - 1):
            lat_forth(c, d).wait_recv()
        line = lrecv[:, c].reshape(m * lat_rows, features)
        result = attend(
            line, wqkv2[:, :split], wvt2[...], wo2[...], lambda h: scales[1, h], heads, None
        )
        lout[:, c] = result.astype(BF16).reshape(m, lat_rows, features)
        for d in range(m - 1):
            lat_back(c, d).start()
        lret[mine, c] = lout[mine, c]

    def finish_lat(c):
        for d in range(m - 1):
            lat_back(c, d).wait_recv()
        for p in range(m):
            total = (state[c, p] + lret[p, c].astype(F32)).astype(BF16).astype(F32)
            place = pl.ds(p * cols_own + c, lat_rows, stride=width)
            for half in range(halves):
                wide.at[half][place, :] = total[:, half * LANES : (half + 1) * LANES]

    finish_lon(0)

    @pl.loop(0, cols_own)
    def _(c):
        @pl.when(c < cols_own - 1)
        def _():
            finish_lon(c + 1)

        lat_line(c)

        @pl.when(c > 0)
        def _():
            finish_lat(c - 1)

    finish_lat(cols_own - 1)

    @pl.loop(0, lat_rows // chunk)
    def _(i):
        place = pl.ds(pl.multiple_of(i * (chunk * width), chunk * width), chunk * width)
        for half in range(halves):
            block = wide[half, place, :].astype(BF16).reshape(chunk, width, LANES)
            out_ref[pl.ds(i * chunk, chunk), :, half * LANES : (half + 1) * LANES] = block

    @pl.loop(0, chunks)
    def _(ch):
        for d in range(n - 1):
            forth(ch, d).wait_send()

    @pl.loop(0, cols_own)
    def _(c):
        for d in range(n - 1):
            back(c, d).wait_send()
        for d in range(m - 1):
            lat_forth(c, d).wait_send()
            lat_back(c, d).wait_send()


def attention(fields, norm_gains, lon_qkv, lon_out, lat_qkv, lat_out, logit_scales):
    lat_rows, lon_cols, features = fields.shape
    heads = logit_scales.shape[1]
    n, m = lax.axis_size("lon"), lax.axis_size("lat")
    width = -(-lon_cols // 16) * 16
    rows_own, cols_own = lat_rows // n, lon_cols // m
    chunk = next(size for size in (4, 3, 2, 1) if rows_own % size == 0)
    chunks, halves = rows_own // chunk, features // LANES
    segment = -(-(m * rows_own) // 16) * 16
    padded = jnp.pad(fields, ((0, 0), (0, width - lon_cols), (0, 0)))
    vmem = pl.BlockSpec(memory_space=pltpu.VMEM)
    dma = pltpu.SemaphoreType.DMA
    return pl.pallas_call(
        functools.partial(attention_kernel, n, m, heads, lon_cols, chunk),
        out_shape=jax.ShapeDtypeStruct((lat_rows, width, features), BF16),
        in_specs=[vmem] * 6 + [pl.BlockSpec(memory_space=pltpu.SMEM)],
        out_specs=vmem,
        scratch_shapes=[
            pltpu.VMEM((n, rows_own, width, features), BF16),
            pltpu.VMEM((n, rows_own, width, features), BF16),
            pltpu.VMEM((halves, lat_rows * width, LANES), F32),
            pltpu.VMEM((halves, n * width * rows_own, LANES), F32),
            pltpu.VMEM((n, cols_own, segment, features), BF16),
            pltpu.VMEM((n, cols_own, segment, features), BF16),
            pltpu.VMEM((cols_own, m, lat_rows, features), F32),
            pltpu.VMEM((m, cols_own, lat_rows, features), BF16),
            pltpu.VMEM((m, cols_own, lat_rows, features), BF16),
            pltpu.VMEM((m, cols_own, lat_rows, features), BF16),
            pltpu.VMEM((m, cols_own, lat_rows, features), BF16),
            pltpu.VMEM((features, features), BF16),
            pltpu.VMEM((features, features), BF16),
            dma((chunks, n - 1)), dma((chunks, n - 1)),
            dma((cols_own, n - 1)), dma((cols_own, n - 1)),
            dma((cols_own, m - 1)), dma((cols_own, m - 1)),
            dma((cols_own, m - 1)), dma((cols_own, m - 1)),
        ],
        compiler_params=pltpu.CompilerParams(
            collective_id=0, has_side_effects=True, vmem_limit_bytes=60 * 2**20
        ),
    )(padded, norm_gains, lon_qkv, lon_out, lat_qkv, lat_out, logit_scales)


def mixer_kernel(rows, lon_cols, wide, taps, gains, w_in, w_down, out):
    step = pl.program_id(0)
    width, features = wide.shape[1], wide.shape[2]
    hidden_len = w_down.shape[0]
    margin = KERNEL // 2
    lines = wide[pl.ds(step * rows, rows + 2 * margin)].astype(F32)
    smoothed = None
    for dx in range(KERNEL):
        term = None
        for dy in range(KERNEL):
            tap = taps[pl.ds(dy * KERNEL + dx, 1), :][None]
            piece = tap * lines[dy : dy + rows]
            term = piece if term is None else term + piece
        if dx:
            term = pltpu.roll(term, width - dx, 1)
        smoothed = term if smoothed is None else smoothed + term
    normed = layer_norm(smoothed.reshape(rows * width, features), gains[2:3]).astype(BF16)
    gate_up = jnp.dot(normed, w_in[...], preferred_element_type=F32)
    half = gate_up[:, :hidden_len] * 0.5
    hidden = (half * (1.0 + jnp.tanh(half)) * gate_up[:, hidden_len:]).astype(BF16)
    update = jnp.dot(hidden, w_down[...], preferred_element_type=F32)
    centre = pltpu.roll(lines[margin : margin + rows], width - margin, 1)
    total = centre + update.reshape(rows, width, features)
    out[...] = total[:, :lon_cols].astype(BF16)


def mixer(second, conv_taps, norm_gains, mlp_in, mlp_down):
    lat_rows, lon_cols, features = second.shape
    margin = KERNEL // 2
    widened = extended(second, (("lon", 1),), margin, True)
    widened = extended(widened, (("lat", 0),), margin, False)
    width = -(-widened.shape[1] // 16) * 16
    widened = jnp.pad(widened, ((0, 0), (0, width - widened.shape[1]), (0, 0)))
    rows = next(r for r in (8, 6, 4, 3, 2, 1) if lat_rows % r == 0)
    vmem = pl.BlockSpec(memory_space=pltpu.VMEM)
    return pl.pallas_call(
        functools.partial(mixer_kernel, rows, lon_cols),
        grid=(lat_rows // rows,),
        out_shape=jax.ShapeDtypeStruct((lat_rows, lon_cols, features), BF16),
        in_specs=[vmem] * 5,
        out_specs=pl.BlockSpec((rows, lon_cols, features), lambda i: (i, 0, 0)),
        compiler_params=pltpu.CompilerParams(vmem_limit_bytes=48 * 2**20),
    )(widened, conv_taps, norm_gains, mlp_in, mlp_down)


def per_device(
    fields, norm_gains, lon_qkv, lon_out, lat_qkv, lat_out, logit_scales, conv_taps, mlp_in, mlp_down
):
    lon_cols = fields.shape[1]
    second = attention(fields, norm_gains, lon_qkv, lon_out, lat_qkv, lat_out, logit_scales)
    return mixer(second[:, :lon_cols], conv_taps, norm_gains, mlp_in, mlp_down)


def solution(mesh):
    in_specs = (P(("groups", "lat"), "lon", None), P(), P(), P(), P(), P(), P(), P(), P(), P())
    out_specs = P(("groups", "lat"), "lon", None)
    return jax.shard_map(
        per_device, mesh=mesh, in_specs=in_specs, out_specs=out_specs, check_vma=False
    )
```

```python
import functools
import math

import jax
import jax.numpy as jnp
from jax import lax
from jax.experimental import pallas as pl
from jax.experimental.pallas import tpu as pltpu
from jax.sharding import PartitionSpec as P

KERNEL = 5
LANES = 128
EPSILON = 1e-05
MESH = pl.DeviceIdType.MESH
F32, BF16 = jnp.float32, jnp.bfloat16
NT = (((1,), (1,)), ((), ()))
TN = (((0,), (0,)), ((), ()))


def layer_norm(values, gains):
    average = jnp.mean(values, -1, keepdims=True)
    centred = values - average
    spread = jnp.mean(centred * centred, -1, keepdims=True)
    return centred * lax.rsqrt(spread + EPSILON) * gains


def attend(x, wqk, wvt, wout, factor_of, heads, valid):
    features = x.shape[-1]
    size = features // heads
    qk = jnp.dot(x, wqk, preferred_element_type=F32).astype(BF16)
    queries, keys = qk[:, :features], qk[:, features:]
    values = lax.dot_general(wvt, x, NT, preferred_element_type=F32).astype(BF16)
    lane = lax.broadcasted_iota(jnp.int32, (1, features), 1) // size
    parts = []
    for h in range(heads):
        own = keys * (lane == h).astype(F32).astype(BF16)
        scores = lax.dot_general(own, queries, NT, preferred_element_type=F32)
        if valid is not None:
            scores = jnp.where(valid, scores, -1e30)
        top = jnp.max(scores, 0, keepdims=True)
        weights = jnp.exp2((scores - top) * (factor_of(h) * math.log2(math.e)))
        total = jnp.sum(weights, 0, keepdims=True)
        part = jnp.dot(
            values[h * size : (h + 1) * size], weights.astype(BF16), preferred_element_type=F32
        )
        parts.append(part / total)
    context = jnp.concatenate(parts, 0).astype(BF16)
    return lax.dot_general(context, wout, TN, preferred_element_type=F32)


def attention_kernel(
    n, m, heads, lon_cols, chunk,
    x_ref, gains, wqkv1, wo1, wqkv2, wo2, scales,
    out_ref,
    xs, recv, wide, mixed, obuf, ret, state, lsend, lrecv, lout, lret, wvt1, wvt2, esend, erecv, hrecv,
    fs, fr, bs, br, gs, gr, hs, hr, es, er, rs, rr,
):
    rows_own = xs.shape[1]
    width, features = xs.shape[2], xs.shape[3]
    chunks = rows_own // chunk
    lat_rows = rows_own * n
    cols_own = lon_cols // m
    halves = features // LANES
    split = 2 * features
    segment = obuf.shape[2]
    me = lax.axis_index("lon")
    mine = lax.axis_index("lat")
    lon_peers = [lax.rem(me + d, n) for d in range(1, n)]
    lat_peers = [lax.rem(mine + d, m) for d in range(1, m)]

    barrier = pltpu.get_barrier_semaphore()
    for peer in lon_peers:
        pl.semaphore_signal(barrier, inc=1, device_id={"lon": peer}, device_id_type=MESH)
    for peer in lat_peers:
        pl.semaphore_signal(barrier, inc=1, device_id={"lat": peer}, device_id_type=MESH)
    pl.semaphore_wait(barrier, n + m - 2)

    def forth(ch, d):
        peer = lon_peers[d]
        part = pl.ds(ch * chunk, chunk)
        return pltpu.make_async_remote_copy(
            src_ref=xs.at[peer, part], dst_ref=recv.at[me, part],
            send_sem=fs.at[ch, d], recv_sem=fr.at[ch, d],
            device_id={"lon": peer}, device_id_type=MESH,
        )

    def back(c, d):
        peer = lon_peers[d]
        return pltpu.make_async_remote_copy(
            src_ref=obuf.at[peer, c], dst_ref=ret.at[me, c],
            send_sem=bs.at[c, d], recv_sem=br.at[c, d],
            device_id={"lon": peer}, device_id_type=MESH,
        )

    def lat_forth(c, d):
        peer = lat_peers[d]
        return pltpu.make_async_remote_copy(
            src_ref=lsend.at[peer, c], dst_ref=lrecv.at[mine, c],
            send_sem=gs.at[c, d], recv_sem=gr.at[c, d],
            device_id={"lat": peer}, device_id_type=MESH,
        )

    def lat_back(c, d):
        peer = lat_peers[d]
        return pltpu.make_async_remote_copy(
            src_ref=lout.at[peer, c], dst_ref=lret.at[mine, c],
            send_sem=hs.at[c, d], recv_sem=hr.at[c, d],
            device_id={"lat": peer}, device_id_type=MESH,
        )

    margin = KERNEL // 2
    left, right = lax.rem(me + n - 1, n), lax.rem(me + 1, n)
    above, below = lax.rem(mine + m - 1, m), lax.rem(mine + 1, m)

    def edge(side):
        return pltpu.make_async_remote_copy(
            src_ref=esend.at[side], dst_ref=erecv.at[1 - side],
            send_sem=es.at[side], recv_sem=er.at[1 - side],
            device_id={"lon": (left, right)[side]}, device_id_type=MESH,
        )

    def border(side):
        start = (margin, lat_rows)[side]
        return pltpu.make_async_remote_copy(
            src_ref=out_ref.at[pl.ds(start, margin)], dst_ref=hrecv.at[1 - side],
            send_sem=rs.at[side], recv_sem=rr.at[1 - side],
            device_id={"lat": (above, below)[side]}, device_id_type=MESH,
        )

    def rows_of(first, count):
        block = x_ref[pl.ds(first, count)].astype(F32)
        spare_cols = jnp.zeros((count, width - lon_cols, features), F32)
        return jnp.concatenate([block, spare_cols], 1)

    def send_edges():
        for side, base in enumerate((margin, lon_cols)):
            for k in range(margin):
                for half in range(halves):
                    column = wide.at[half][pl.ds(base + k, lat_rows, stride=width), :]
                    esend[side, k, :, half * LANES : (half + 1) * LANES] = column.astype(BF16)
            edge(side).start()

    @pl.loop(0, chunks)
    def _(ch):
        part = pl.ds(ch * chunk, chunk)
        for o in range(n):
            first_row = o * rows_own + ch * chunk
            block = rows_of(first_row, chunk)
            xs[o, part] = layer_norm(block, gains[0:1][None]).astype(BF16)
        for d in range(n - 1):
            forth(ch, d).start()
        recv[me, part] = xs[me, part]

    wvt1[...] = wqkv1[:, split:].astype(F32).T.astype(BF16)
    wvt2[...] = wqkv2[:, split:].astype(F32).T.astype(BF16)

    @pl.loop(0, lat_rows // chunk)
    def _(i):
        block = rows_of(i * chunk, chunk).reshape(chunk * width, features)
        place = pl.ds(pl.multiple_of(i * (chunk * width), chunk * width), chunk * width)
        for half in range(halves):
            wide[half, place, :] = block[:, half * LANES : (half + 1) * LANES]

    @pl.loop(0, cols_own)
    def _(c):
        for p in range(m):
            for half in range(halves):
                place = pl.ds(p * cols_own + c, lat_rows, stride=width)
                state[c, p, :, half * LANES : (half + 1) * LANES] = wide.at[half][place, :]

    position = lax.broadcasted_iota(jnp.int32, (n * width, 1), 0)
    valid = lax.rem(position, width) < lon_cols

    @pl.loop(0, chunks)
    def _(ch):
        for d in range(n - 1):
            forth(ch, d).wait_recv()

        @pl.loop(0, chunk)
        def _(i):
            row = ch * chunk + i
            line = recv[:, row].reshape(n * width, features)
            result = attend(
                line, wqkv1[:, :split], wvt1[...], wo1[...], lambda h: scales[0, h], heads, valid
            )
            place = pl.ds(row, n * width, stride=rows_own)
            for half in range(halves):
                mixed.at[half][place, :] = result[:, half * LANES : (half + 1) * LANES]

    spare = segment - m * rows_own

    def group(t):
        return lax.rem(t + (cols_own - margin), cols_own)

    @pl.loop(0, cols_own)
    def _(t):
        c = group(t)
        for j in range(n):
            for half in range(halves):
                pieces = []
                for p in range(m):
                    start = (j * width + p * cols_own + c) * rows_own
                    if rows_own % 8 == 0:
                        start = pl.multiple_of(start, 8)
                    pieces.append(mixed[half, pl.ds(start, rows_own), :])
                if spare:
                    pieces.append(jnp.zeros((spare, LANES), F32))
                block = jnp.concatenate(pieces, 0).astype(BF16)
                obuf[j, c, :, half * LANES : (half + 1) * LANES] = block
        for d in range(n - 1):
            back(c, d).start()
        ret[me, c] = obuf[me, c]

    def finish_lon(c):
        for d in range(n - 1):
            back(c, d).wait_recv()
        arrived = [ret[o, c].astype(F32) for o in range(n)]
        for p in range(m):
            lon_mix = jnp.concatenate(
                [block[p * rows_own : (p + 1) * rows_own] for block in arrived], 0
            )
            first = (state[c, p] + lon_mix).astype(BF16).astype(F32)
            state[c, p] = first
            lsend[p, c] = layer_norm(first, gains[1:2]).astype(BF16)
        for d in range(m - 1):
            lat_forth(c, d).start()
        lrecv[mine, c] = lsend[mine, c]

    def lat_line(c):
        for d in range(m - 1):
            lat_forth(c, d).wait_recv()
        line = lrecv[:, c].reshape(m * lat_rows, features)
        result = attend(
            line, wqkv2[:, :split], wvt2[...], wo2[...], lambda h: scales[1, h], heads, None
        )
        lout[:, c] = result.astype(BF16).reshape(m, lat_rows, features)
        for d in range(m - 1):
            lat_back(c, d).start()
        lret[mine, c] = lout[mine, c]

    def finish_lat(c):
        for d in range(m - 1):
            lat_back(c, d).wait_recv()
        for p in range(m):
            total = (state[c, p] + lret[p, c].astype(F32)).astype(BF16).astype(F32)
            place = pl.ds(margin + p * cols_own + c, lat_rows, stride=width)
            for half in range(halves):
                wide.at[half][place, :] = total[:, half * LANES : (half + 1) * LANES]

    finish_lon(group(0))

    @pl.loop(0, cols_own)
    def _(t):
        @pl.when(t < cols_own - 1)
        def _():
            finish_lon(group(t + 1))

        lat_line(group(t))

        @pl.when(t > 0)
        def _():
            finish_lat(group(t - 1))

        if cols_own > 2 * margin:

            @pl.when(t == 2 * margin)
            def _():
                send_edges()

    finish_lat(group(cols_own - 1))
    if cols_own <= 2 * margin:
        send_edges()

    for side, base in enumerate((0, margin + lon_cols)):
        edge(1 - side).wait_recv()
        for k in range(margin):
            for half in range(halves):
                column = erecv[side, k, :, half * LANES : (half + 1) * LANES].astype(F32)
                wide.at[half][pl.ds(base + k, lat_rows, stride=width), :] = column

    def emit(first, count):
        place = pl.ds(first * width, count * width)
        for half in range(halves):
            block = wide[half, place, :].astype(BF16).reshape(count, width, LANES)
            out_ref[pl.ds(margin + first, count), :, half * LANES : (half + 1) * LANES] = block

    ends = (mine > 0, mine < m - 1)
    for side, first in enumerate((0, lat_rows - margin)):
        emit(first, margin)

        @pl.when(ends[side])
        def _():
            border(side).start()

    count = next(size for size in (4, 2, 1) if (lat_rows - 2 * margin) % size == 0)

    @pl.loop(0, (lat_rows - 2 * margin) // count)
    def _(i):
        first = margin + i * count
        place = pl.ds(pl.multiple_of(first * width, width), count * width)
        for half in range(halves):
            block = wide[half, place, :].astype(BF16).reshape(count, width, LANES)
            out_ref[pl.ds(margin + first, count), :, half * LANES : (half + 1) * LANES] = block

    for side, first in enumerate((0, margin + lat_rows)):

        @pl.when(ends[side])
        def _():
            border(1 - side).wait_recv()
            out_ref[pl.ds(first, margin)] = hrecv[side]

        @pl.when(jnp.logical_not(ends[side]))
        def _():
            out_ref[pl.ds(first, margin)] = jnp.zeros((margin, width, features), BF16)

    for side in range(2):
        edge(side).wait_send()

        @pl.when(ends[side])
        def _():
            border(side).wait_send()

    @pl.loop(0, chunks)
    def _(ch):
        for d in range(n - 1):
            forth(ch, d).wait_send()

    @pl.loop(0, cols_own)
    def _(c):
        for d in range(n - 1):
            back(c, d).wait_send()
        for d in range(m - 1):
            lat_forth(c, d).wait_send()
            lat_back(c, d).wait_send()


def attention(fields, norm_gains, lon_qkv, lon_out, lat_qkv, lat_out, logit_scales):
    lat_rows, lon_cols, features = fields.shape
    heads = logit_scales.shape[1]
    n, m = lax.axis_size("lon"), lax.axis_size("lat")
    margin = KERNEL // 2
    width = -(-(lon_cols + 2 * margin) // 16) * 16
    rows_own, cols_own = lat_rows // n, lon_cols // m
    chunk = next(size for size in (4, 3, 2, 1) if rows_own % size == 0)
    chunks, halves = rows_own // chunk, features // LANES
    segment = -(-(m * rows_own) // 16) * 16
    vmem = pl.BlockSpec(memory_space=pltpu.VMEM)
    dma = pltpu.SemaphoreType.DMA
    return pl.pallas_call(
        functools.partial(attention_kernel, n, m, heads, lon_cols, chunk),
        out_shape=jax.ShapeDtypeStruct((lat_rows + 2 * margin, width, features), BF16),
        in_specs=[vmem] * 6 + [pl.BlockSpec(memory_space=pltpu.SMEM)],
        out_specs=vmem,
        scratch_shapes=[
            pltpu.VMEM((n, rows_own, width, features), BF16),
            pltpu.VMEM((n, rows_own, width, features), BF16),
            pltpu.VMEM((halves, lat_rows * width, LANES), F32),
            pltpu.VMEM((halves, n * width * rows_own, LANES), F32),
            pltpu.VMEM((n, cols_own, segment, features), BF16),
            pltpu.VMEM((n, cols_own, segment, features), BF16),
            pltpu.VMEM((cols_own, m, lat_rows, features), F32),
            pltpu.VMEM((m, cols_own, lat_rows, features), BF16),
            pltpu.VMEM((m, cols_own, lat_rows, features), BF16),
            pltpu.VMEM((m, cols_own, lat_rows, features), BF16),
            pltpu.VMEM((m, cols_own, lat_rows, features), BF16),
            pltpu.VMEM((features, features), BF16),
            pltpu.VMEM((features, features), BF16),
            pltpu.VMEM((2, margin, lat_rows, features), BF16),
            pltpu.VMEM((2, margin, lat_rows, features), BF16),
            pltpu.VMEM((2, margin, width, features), BF16),
            dma((chunks, n - 1)), dma((chunks, n - 1)),
            dma((cols_own, n - 1)), dma((cols_own, n - 1)),
            dma((cols_own, m - 1)), dma((cols_own, m - 1)),
            dma((cols_own, m - 1)), dma((cols_own, m - 1)),
            dma((2,)), dma((2,)), dma((2,)), dma((2,)),
        ],
        compiler_params=pltpu.CompilerParams(
            collective_id=0, has_side_effects=True, vmem_limit_bytes=60 * 2**20
        ),
    )(fields, norm_gains, lon_qkv, lon_out, lat_qkv, lat_out, logit_scales)


def mixer_kernel(rows, lon_cols, wide, taps, gains, w_in, w_down, out):
    step = pl.program_id(0)
    width, features = wide.shape[1], wide.shape[2]
    hidden_len = w_down.shape[0]
    margin = KERNEL // 2
    lines = wide[pl.ds(step * rows, rows + 2 * margin)].astype(F32)
    smoothed = None
    for dx in range(KERNEL):
        term = None
        for dy in range(KERNEL):
            tap = taps[pl.ds(dy * KERNEL + dx, 1), :][None]
            piece = tap * lines[dy : dy + rows]
            term = piece if term is None else term + piece
        if dx:
            term = pltpu.roll(term, width - dx, 1)
        smoothed = term if smoothed is None else smoothed + term
    normed = layer_norm(smoothed.reshape(rows * width, features), gains[2:3]).astype(BF16)
    gate_up = jnp.dot(normed, w_in[...], preferred_element_type=F32)
    half = gate_up[:, :hidden_len] * 0.5
    hidden = (half * (1.0 + jnp.tanh(half)) * gate_up[:, hidden_len:]).astype(BF16)
    update = jnp.dot(hidden, w_down[...], preferred_element_type=F32)
    centre = pltpu.roll(lines[margin : margin + rows], width - margin, 1)
    total = centre + update.reshape(rows, width, features)
    out[...] = total[:, :lon_cols].astype(BF16)


def mixer(widened, lon_cols, conv_taps, norm_gains, mlp_in, mlp_down):
    features = widened.shape[2]
    lat_rows = widened.shape[0] - KERNEL + 1
    rows = next(r for r in (8, 6, 4, 3, 2, 1) if lat_rows % r == 0)
    vmem = pl.BlockSpec(memory_space=pltpu.VMEM)
    return pl.pallas_call(
        functools.partial(mixer_kernel, rows, lon_cols),
        grid=(lat_rows // rows,),
        out_shape=jax.ShapeDtypeStruct((lat_rows, lon_cols, features), BF16),
        in_specs=[vmem] * 5,
        out_specs=pl.BlockSpec((rows, lon_cols, features), lambda i: (i, 0, 0)),
        compiler_params=pltpu.CompilerParams(vmem_limit_bytes=60 * 2**20),
    )(widened, conv_taps, norm_gains, mlp_in, mlp_down)


def per_device(
    fields, norm_gains, lon_qkv, lon_out, lat_qkv, lat_out, logit_scales, conv_taps, mlp_in, mlp_down
):
    lon_cols = fields.shape[1]
    widened = attention(fields, norm_gains, lon_qkv, lon_out, lat_qkv, lat_out, logit_scales)
    return mixer(widened, lon_cols, conv_taps, norm_gains, mlp_in, mlp_down)


def solution(mesh):
    in_specs = (P(("groups", "lat"), "lon", None), P(), P(), P(), P(), P(), P(), P(), P(), P())
    out_specs = P(("groups", "lat"), "lon", None)
    return jax.shard_map(
        per_device, mesh=mesh, in_specs=in_specs, out_specs=out_specs, check_vma=False
    )
```

```python
import functools
import math

import jax
import jax.numpy as jnp
from jax import lax
from jax.experimental import pallas as pl
from jax.experimental.pallas import tpu as pltpu
from jax.sharding import PartitionSpec as P

KERNEL = 5
LANES = 128
EPSILON = 1e-05
MESH = pl.DeviceIdType.MESH
F32, BF16 = jnp.float32, jnp.bfloat16
NT = (((1,), (1,)), ((), ()))
TN = (((0,), (0,)), ((), ()))


def layer_norm(values, gains):
    average = jnp.mean(values, -1, keepdims=True)
    centred = values - average
    spread = jnp.mean(centred * centred, -1, keepdims=True)
    return centred * lax.rsqrt(spread + EPSILON) * gains


def attend(x, wqk, wvt, wout, factor_of, heads):
    features = x.shape[-1]
    size = features // heads
    qk = jnp.dot(x, wqk, preferred_element_type=F32).astype(BF16)
    queries, keys = qk[:, :features], qk[:, features:]
    values = lax.dot_general(wvt, x, NT, preferred_element_type=F32).astype(BF16)
    lane = lax.broadcasted_iota(jnp.int32, (1, features), 1) // size
    parts = []
    for h in range(heads):
        own = keys * (lane == h).astype(F32).astype(BF16)
        scores = lax.dot_general(own, queries, NT, preferred_element_type=F32)
        top = jnp.max(scores, 0, keepdims=True)
        weights = jnp.exp2((scores - top) * (factor_of(h) * math.log2(math.e)))
        total = jnp.sum(weights, 0, keepdims=True)
        part = jnp.dot(
            values[h * size : (h + 1) * size], weights.astype(BF16), preferred_element_type=F32
        )
        parts.append(part / total)
    context = jnp.concatenate(parts, 0).astype(BF16)
    return lax.dot_general(context, wout, TN, preferred_element_type=F32)


def attention_kernel(
    n, m, heads, lon_cols, chunk,
    x_ref, gains, wqkv1, wo1, wqkv2, wo2, scales,
    out_ref, halo_ref,
    xs, recv, normed, stage, lines, mixed, obuf, ret, state, lsend, lrecv, lout, lret, wvt1, wvt2, erecv, rims, hsend, hrecv,
    fs, fr, bs, br, gs, gr, hs, hr, es, er, rs, rr,
):
    lat_rows, features = x_ref.shape[1:]
    rows_own = lat_rows // n
    chunks = rows_own // chunk
    tokens = xs.shape[2]
    slot = tokens // lon_cols
    width = lon_cols + KERNEL - 1
    cols_own = lon_cols // m
    halves = features // LANES
    split = 2 * features
    segment = obuf.shape[2]
    me = lax.axis_index("lon")
    mine = lax.axis_index("lat")
    lon_peers = [lax.rem(me + d, n) for d in range(1, n)]
    lat_peers = [lax.rem(mine + d, m) for d in range(1, m)]

    barrier = pltpu.get_barrier_semaphore()
    for peer in lon_peers:
        pl.semaphore_signal(barrier, inc=1, device_id={"lon": peer}, device_id_type=MESH)
    for peer in lat_peers:
        pl.semaphore_signal(barrier, inc=1, device_id={"lat": peer}, device_id_type=MESH)
    pl.semaphore_wait(barrier, n + m - 2)

    def forth(ch, d):
        peer = lon_peers[d]
        return pltpu.make_async_remote_copy(
            src_ref=xs.at[peer, ch], dst_ref=recv.at[me, ch],
            send_sem=fs.at[ch, d], recv_sem=fr.at[ch, d],
            device_id={"lon": peer}, device_id_type=MESH,
        )

    def back(c, d):
        peer = lon_peers[d]
        return pltpu.make_async_remote_copy(
            src_ref=obuf.at[peer, c], dst_ref=ret.at[me, c],
            send_sem=bs.at[c, d], recv_sem=br.at[c, d],
            device_id={"lon": peer}, device_id_type=MESH,
        )

    def lat_forth(c, d):
        peer = lat_peers[d]
        return pltpu.make_async_remote_copy(
            src_ref=lsend.at[peer, c], dst_ref=lrecv.at[mine, c],
            send_sem=gs.at[c, d], recv_sem=gr.at[c, d],
            device_id={"lat": peer}, device_id_type=MESH,
        )

    def lat_back(c, d):
        peer = lat_peers[d]
        return pltpu.make_async_remote_copy(
            src_ref=lout.at[peer, c], dst_ref=lret.at[mine, c],
            send_sem=hs.at[c, d], recv_sem=hr.at[c, d],
            device_id={"lat": peer}, device_id_type=MESH,
        )

    margin = KERNEL // 2
    left, right = lax.rem(me + n - 1, n), lax.rem(me + 1, n)
    above, below = lax.rem(mine + m - 1, m), lax.rem(mine + 1, m)

    def edge(side):
        start = (margin, lon_cols)[side]
        return pltpu.make_async_remote_copy(
            src_ref=out_ref.at[pl.ds(start, margin)], dst_ref=erecv.at[1 - side],
            send_sem=es.at[side], recv_sem=er.at[1 - side],
            device_id={"lon": (left, right)[side]}, device_id_type=MESH,
        )

    def border(side):
        return pltpu.make_async_remote_copy(
            src_ref=hsend.at[side], dst_ref=hrecv.at[1 - side],
            send_sem=rs.at[side], recv_sem=rr.at[1 - side],
            device_id={"lat": (above, below)[side]}, device_id_type=MESH,
        )

    def lanes(half):
        return slice(half * LANES, (half + 1) * LANES)

    @pl.loop(0, lon_cols)
    def _(col):
        block = layer_norm(x_ref[col].astype(F32), gains[0:1])
        place = pl.ds(pl.multiple_of(col * lat_rows, 8), lat_rows)
        for half in range(halves):
            normed[half, place, :] = block[:, lanes(half)]

    if slot > chunk:
        stage[...] = jnp.zeros(stage.shape, F32)

    @pl.loop(0, chunks)
    def _(ch):
        for o in range(n):
            for half in range(halves):
                for i in range(chunk):
                    row = o * rows_own + ch * chunk + i
                    taken = normed.at[half][pl.ds(row, lon_cols, stride=lat_rows), :]
                    stage.at[o % 2, half][pl.ds(i, lon_cols, stride=slot), :] = taken
                xs[o, ch, :, lanes(half)] = stage[o % 2, half].astype(BF16)
        for d in range(n - 1):
            forth(ch, d).start()
        recv[me, ch] = xs[me, ch]

    wvt1[...] = wqkv1[:, split:].astype(F32).T.astype(BF16)
    wvt2[...] = wqkv2[:, split:].astype(F32).T.astype(BF16)

    @pl.loop(0, chunks)
    def _(ch):
        for d in range(n - 1):
            forth(ch, d).wait_recv()
        for j in range(n):
            for half in range(halves):
                arrived = recv[j, ch, :, lanes(half)].astype(F32)
                lines[half, j * tokens : (j + 1) * tokens, :] = arrived

        @pl.loop(0, chunk)
        def _(i):
            place = pl.ds(i, n * lon_cols, stride=slot)
            line = jnp.concatenate(
                [lines.at[half][place, :] for half in range(halves)], 1
            ).astype(BF16)
            result = attend(
                line, wqkv1[:, :split], wvt1[...], wo1[...], lambda h: scales[0, h], heads
            )
            place = pl.ds(ch * chunk + i, n * lon_cols, stride=rows_own)
            for half in range(halves):
                mixed.at[half][place, :] = result[:, lanes(half)]

    spare = segment - m * rows_own

    def group(t):
        return lax.rem(t + (cols_own - margin), cols_own)

    @pl.loop(0, cols_own)
    def _(t):
        c = group(t)
        for j in range(n):
            for half in range(halves):
                pieces = []
                for p in range(m):
                    start = (j * lon_cols + p * cols_own + c) * rows_own
                    if rows_own % 8 == 0:
                        start = pl.multiple_of(start, 8)
                    pieces.append(mixed[half, pl.ds(start, rows_own), :])
                if spare:
                    pieces.append(jnp.zeros((spare, LANES), F32))
                block = jnp.concatenate(pieces, 0).astype(BF16)
                obuf[j, c, :, lanes(half)] = block
        for d in range(n - 1):
            back(c, d).start()
        ret[me, c] = obuf[me, c]

    def finish_lon(c):
        for d in range(n - 1):
            back(c, d).wait_recv()
        arrived = [ret[o, c].astype(F32) for o in range(n)]
        for p in range(m):
            lon_mix = jnp.concatenate(
                [block[p * rows_own : (p + 1) * rows_own] for block in arrived], 0
            )
            first = (x_ref[p * cols_own + c].astype(F32) + lon_mix).astype(BF16).astype(F32)
            state[c, p] = first
            lsend[p, c] = layer_norm(first, gains[1:2]).astype(BF16)
        for d in range(m - 1):
            lat_forth(c, d).start()
        lrecv[mine, c] = lsend[mine, c]

    def lat_line(c):
        for d in range(m - 1):
            lat_forth(c, d).wait_recv()
        line = lrecv[:, c].reshape(m * lat_rows, features)
        result = attend(
            line, wqkv2[:, :split], wvt2[...], wo2[...], lambda h: scales[1, h], heads
        )
        lout[:, c] = result.astype(BF16).reshape(m, lat_rows, features)
        for d in range(m - 1):
            lat_back(c, d).start()
        lret[mine, c] = lout[mine, c]

    def keep_rims(col, block):
        place = pl.ds(pl.multiple_of(col * 8, 8), 8)
        for half in range(halves):
            rims[0, half, place, :] = block[:8, lanes(half)]
            rims[1, half, place, :] = block[lat_rows - 8 :, lanes(half)]

    def finish_lat(c):
        for d in range(m - 1):
            lat_back(c, d).wait_recv()
        for p in range(m):
            total = (state[c, p] + lret[p, c].astype(F32)).astype(BF16)
            col = margin + p * cols_own + c
            out_ref[col] = total
            keep_rims(col, total.astype(F32))

    finish_lon(group(0))

    @pl.loop(0, cols_own)
    def _(t):
        @pl.when(t < cols_own - 1)
        def _():
            finish_lon(group(t + 1))

        lat_line(group(t))

        @pl.when(t > 0)
        def _():
            finish_lat(group(t - 1))

        if cols_own > 2 * margin:

            @pl.when(t == 2 * margin)
            def _():
                for side in range(2):
                    edge(side).start()

    finish_lat(group(cols_own - 1))
    if cols_own <= 2 * margin:
        for side in range(2):
            edge(side).start()

    for side, base in enumerate((0, margin + lon_cols)):
        edge(1 - side).wait_recv()
        for k in range(margin):
            out_ref[base + k] = erecv[side, k]
            keep_rims(base + k, erecv[side, k].astype(F32))

    ends = (mine > 0, mine < m - 1)
    for side, base in enumerate((0, 8 - margin)):
        for k in range(margin):
            for half in range(halves):
                row = rims.at[side, half][pl.ds(base + k, width, stride=8), :]
                hsend[side, k, :, lanes(half)] = row.astype(BF16)

        @pl.when(ends[side])
        def _():
            border(side).start()

    halo_ref[...] = jnp.zeros(halo_ref.shape, F32)
    for side, base in enumerate((8 - margin, 0)):

        @pl.when(ends[side])
        def _():
            border(1 - side).wait_recv()
            for k in range(margin):
                for half in range(halves):
                    row = hrecv[side, k, :, lanes(half)].astype(F32)
                    halo_ref.at[side, half][pl.ds(base + k, width, stride=8), :] = row

    for side in range(2):
        edge(side).wait_send()

        @pl.when(ends[side])
        def _():
            border(side).wait_send()

    @pl.loop(0, chunks)
    def _(ch):
        for d in range(n - 1):
            forth(ch, d).wait_send()

    @pl.loop(0, cols_own)
    def _(c):
        for d in range(n - 1):
            back(c, d).wait_send()
        for d in range(m - 1):
            lat_forth(c, d).wait_send()
            lat_back(c, d).wait_send()


def attention(fields, norm_gains, lon_qkv, lon_out, lat_qkv, lat_out, logit_scales):
    lon_cols, lat_rows, features = fields.shape
    heads = logit_scales.shape[1]
    n, m = lax.axis_size("lon"), lax.axis_size("lat")
    margin = KERNEL // 2
    width = lon_cols + 2 * margin
    rows_own, cols_own = lat_rows // n, lon_cols // m
    chunk = next(size for size in (4, 3, 2, 1) if rows_own % size == 0)
    slot = chunk
    while lon_cols * slot % 16:
        slot += 1
    tokens = lon_cols * slot
    chunks, halves = rows_own // chunk, features // LANES
    segment = -(-(m * rows_own) // 16) * 16
    vmem = pl.BlockSpec(memory_space=pltpu.VMEM)
    dma = pltpu.SemaphoreType.DMA
    groups = (m, cols_own, lat_rows, features)
    return pl.pallas_call(
        functools.partial(attention_kernel, n, m, heads, lon_cols, chunk),
        out_shape=(
            jax.ShapeDtypeStruct((width, lat_rows, features), BF16),
            jax.ShapeDtypeStruct((2, halves, width * 8, LANES), F32),
        ),
        in_specs=[vmem] * 6 + [pl.BlockSpec(memory_space=pltpu.SMEM)],
        out_specs=(vmem, vmem),
        scratch_shapes=[
            pltpu.VMEM((n, chunks, tokens, features), BF16),
            pltpu.VMEM((n, chunks, tokens, features), BF16),
            pltpu.VMEM((halves, lon_cols * lat_rows, LANES), F32),
            pltpu.VMEM((2, halves, tokens, LANES), F32),
            pltpu.VMEM((halves, n * tokens, LANES), F32),
            pltpu.VMEM((halves, n * lon_cols * rows_own, LANES), F32),
            pltpu.VMEM((n, cols_own, segment, features), BF16),
            pltpu.VMEM((n, cols_own, segment, features), BF16),
            pltpu.VMEM((cols_own, m, lat_rows, features), F32),
            pltpu.VMEM(groups, BF16),
            pltpu.VMEM(groups, BF16),
            pltpu.VMEM(groups, BF16),
            pltpu.VMEM(groups, BF16),
            pltpu.VMEM((features, features), BF16),
            pltpu.VMEM((features, features), BF16),
            pltpu.VMEM((2, margin, lat_rows, features), BF16),
            pltpu.VMEM((2, halves, width * 8, LANES), F32),
            pltpu.VMEM((2, margin, width, features), BF16),
            pltpu.VMEM((2, margin, width, features), BF16),
            dma((chunks, n - 1)), dma((chunks, n - 1)),
            dma((cols_own, n - 1)), dma((cols_own, n - 1)),
            dma((cols_own, m - 1)), dma((cols_own, m - 1)),
            dma((cols_own, m - 1)), dma((cols_own, m - 1)),
            dma((2,)), dma((2,)), dma((2,)), dma((2,)),
        ],
        compiler_params=pltpu.CompilerParams(
            collective_id=0, has_side_effects=True, vmem_limit_bytes=60 * 2**20
        ),
    )(fields, norm_gains, lon_qkv, lon_out, lat_qkv, lat_out, logit_scales)


def mixer_kernel(cols, wide, halo, taps, gains, w_in, w_down, out):
    first = pl.program_id(0) * cols
    rows, features = wide.shape[1:]
    hidden_len = w_down.shape[0]
    margin = KERNEL // 2
    count = cols + 2 * margin
    body = wide[pl.ds(first, count)].astype(F32)
    place = pl.ds(pl.multiple_of(first * 8, 8), count * 8)
    rims = [
        jnp.concatenate([halo[side, half, place, :] for half in range(features // LANES)], 1)
        for side in range(2)
    ]
    rims = [rim.reshape(count, 8, features) for rim in rims]
    lines = jnp.concatenate([rims[0], body, rims[1]], 1)
    smoothed = None
    for dy in range(KERNEL):
        term = None
        for dx in range(KERNEL):
            tap = taps[pl.ds(dy * KERNEL + dx, 1), :][None]
            piece = tap * lines[dx : dx + cols]
            term = piece if term is None else term + piece
        term = term[:, 8 - margin + dy : 8 - margin + dy + rows]
        smoothed = term if smoothed is None else smoothed + term
    normed = layer_norm(smoothed.reshape(cols * rows, features), gains[2:3]).astype(BF16)
    gate_up = jnp.dot(normed, w_in[...], preferred_element_type=F32)
    half = gate_up[:, :hidden_len] * 0.5
    hidden = (half * (1.0 + jnp.tanh(half)) * gate_up[:, hidden_len:]).astype(BF16)
    update = jnp.dot(hidden, w_down[...], preferred_element_type=F32)
    total = body[margin : margin + cols] + update.reshape(cols, rows, features)
    out[...] = total.astype(BF16)


def mixer(widened, halo, conv_taps, norm_gains, mlp_in, mlp_down):
    width, lat_rows, features = widened.shape
    lon_cols = width - KERNEL + 1
    cols = next(size for size in (4, 3, 2, 1) if lon_cols % size == 0)
    vmem = pl.BlockSpec(memory_space=pltpu.VMEM)
    return pl.pallas_call(
        functools.partial(mixer_kernel, cols),
        grid=(lon_cols // cols,),
        out_shape=jax.ShapeDtypeStruct((lon_cols, lat_rows, features), BF16),
        in_specs=[vmem] * 6,
        out_specs=pl.BlockSpec((cols, lat_rows, features), lambda i: (i, 0, 0)),
        compiler_params=pltpu.CompilerParams(vmem_limit_bytes=60 * 2**20),
    )(widened, halo, conv_taps, norm_gains, mlp_in, mlp_down)


def per_device(
    fields, norm_gains, lon_qkv, lon_out, lat_qkv, lat_out, logit_scales, conv_taps, mlp_in, mlp_down
):
    columns = jnp.swapaxes(fields, 0, 1)
    widened, halo = attention(
        columns, norm_gains, lon_qkv, lon_out, lat_qkv, lat_out, logit_scales
    )
    return jnp.swapaxes(mixer(widened, halo, conv_taps, norm_gains, mlp_in, mlp_down), 0, 1)


def solution(mesh):
    in_specs = (P(("groups", "lat"), "lon", None), P(), P(), P(), P(), P(), P(), P(), P(), P())
    out_specs = P(("groups", "lat"), "lon", None)
    return jax.shard_map(
        per_device, mesh=mesh, in_specs=in_specs, out_specs=out_specs, check_vma=False
    )
```

```python
import functools
import math

import jax
import jax.numpy as jnp
from jax import lax
from jax.experimental import pallas as pl
from jax.experimental.pallas import tpu as pltpu
from jax.sharding import PartitionSpec as P

KERNEL = 5
LANES = 128
EPSILON = 1e-05
MESH = pl.DeviceIdType.MESH
F32, BF16 = jnp.float32, jnp.bfloat16
NT = (((1,), (1,)), ((), ()))
TN = (((0,), (0,)), ((), ()))


def layer_norm(values, gains):
    average = jnp.mean(values, -1, keepdims=True)
    centred = values - average
    spread = jnp.mean(centred * centred, -1, keepdims=True)
    return centred * lax.rsqrt(spread + EPSILON) * gains


def attend(lines, wk, wqvt, wout, factors, heads):
    length, features = lines[0].shape
    size = features // heads
    together = max(1, min(heads, 5 * 2**20 // (4 * length * length)))
    lane = lax.broadcasted_iota(jnp.int32, (1, features), 1) // size
    masks = [(lane == h).astype(F32).astype(BF16) for h in range(heads)]
    all_keys = jnp.dot(jnp.concatenate(lines, 0), wk, preferred_element_type=F32).astype(BF16)
    contexts = []
    for number, x in enumerate(lines):
        keys = all_keys[number * length : (number + 1) * length]
        qvt = lax.dot_general(wqvt, x, NT, preferred_element_type=F32).astype(BF16)
        queries, values = qvt[:features], qvt[features:]
        parts = []
        for base in range(0, heads, together):
            group = range(base, min(heads, base + together))
            own = jnp.concatenate([keys * masks[h] for h in group], 0)
            scores = jnp.dot(own, queries, preferred_element_type=F32)
            for h in group:
                score = scores[(h - base) * length : (h - base + 1) * length]
                top = jnp.max(score, 0, keepdims=True)
                weights = jnp.exp2((score - top) * factors[h])
                total = jnp.sum(weights, 0, keepdims=True)
                part = jnp.dot(
                    values[h * size : (h + 1) * size],
                    weights.astype(BF16),
                    preferred_element_type=F32,
                )
                parts.append(part * (1.0 / total))
        contexts.append(jnp.concatenate(parts, 0).astype(BF16).T)
    return jnp.dot(jnp.concatenate(contexts, 0), wout, preferred_element_type=F32)


def attention_kernel(
    n, m, heads, lon_cols, chunk,
    x_ref, gains, wqkv1, wo1, wqkv2, wo2, scales,
    out_ref, halo_ref,
    xs, recv, normed, stage, lines, mixed, obuf, ret, state, lsend, lrecv, lout, lret, wqvt1, wqvt2, erecv, rims, hsend, hrecv,
    fs, fr, bs, br, gs, gr, hs, hr, es, er, rs, rr,
):
    lat_rows, features = x_ref.shape[1:]
    rows_own = lat_rows // n
    chunks = rows_own // chunk
    tokens = xs.shape[2]
    slot = tokens // lon_cols
    width = lon_cols + KERNEL - 1
    cols_own = lon_cols // m
    halves = features // LANES
    split = 2 * features
    segment = obuf.shape[2]
    me = lax.axis_index("lon")
    mine = lax.axis_index("lat")
    lon_peers = [lax.rem(me + d, n) for d in range(1, n)]
    lat_peers = [lax.rem(mine + d, m) for d in range(1, m)]

    barrier = pltpu.get_barrier_semaphore()
    for peer in lon_peers:
        pl.semaphore_signal(barrier, inc=1, device_id={"lon": peer}, device_id_type=MESH)
    for peer in lat_peers:
        pl.semaphore_signal(barrier, inc=1, device_id={"lat": peer}, device_id_type=MESH)
    pl.semaphore_wait(barrier, n + m - 2)

    def forth(ch, d):
        peer = lon_peers[d]
        return pltpu.make_async_remote_copy(
            src_ref=xs.at[peer, ch], dst_ref=recv.at[me, ch],
            send_sem=fs.at[ch, d], recv_sem=fr.at[ch, d],
            device_id={"lon": peer}, device_id_type=MESH,
        )

    def back(c, d):
        peer = lon_peers[d]
        return pltpu.make_async_remote_copy(
            src_ref=obuf.at[peer, c], dst_ref=ret.at[me, c],
            send_sem=bs.at[c, d], recv_sem=br.at[c, d],
            device_id={"lon": peer}, device_id_type=MESH,
        )

    def lat_forth(c, d):
        peer = lat_peers[d]
        return pltpu.make_async_remote_copy(
            src_ref=lsend.at[peer, c], dst_ref=lrecv.at[mine, c],
            send_sem=gs.at[c, d], recv_sem=gr.at[c, d],
            device_id={"lat": peer}, device_id_type=MESH,
        )

    def lat_back(c, d):
        peer = lat_peers[d]
        return pltpu.make_async_remote_copy(
            src_ref=lout.at[peer, c], dst_ref=lret.at[mine, c],
            send_sem=hs.at[c, d], recv_sem=hr.at[c, d],
            device_id={"lat": peer}, device_id_type=MESH,
        )

    margin = KERNEL // 2
    left, right = lax.rem(me + n - 1, n), lax.rem(me + 1, n)
    above, below = lax.rem(mine + m - 1, m), lax.rem(mine + 1, m)

    def edge(side):
        start = (margin, lon_cols)[side]
        return pltpu.make_async_remote_copy(
            src_ref=out_ref.at[pl.ds(start, margin)], dst_ref=erecv.at[1 - side],
            send_sem=es.at[side], recv_sem=er.at[1 - side],
            device_id={"lon": (left, right)[side]}, device_id_type=MESH,
        )

    def border(side):
        return pltpu.make_async_remote_copy(
            src_ref=hsend.at[side], dst_ref=hrecv.at[1 - side],
            send_sem=rs.at[side], recv_sem=rr.at[1 - side],
            device_id={"lat": (above, below)[side]}, device_id_type=MESH,
        )

    def lanes(half):
        return slice(half * LANES, (half + 1) * LANES)

    @pl.loop(0, lon_cols)
    def _(col):
        block = layer_norm(x_ref[col].astype(F32), gains[0:1])
        place = pl.ds(pl.multiple_of(col * lat_rows, 8), lat_rows)
        for half in range(halves):
            normed[half, place, :] = block[:, lanes(half)]

    if slot > chunk:
        stage[...] = jnp.zeros(stage.shape, F32)

    @pl.loop(0, chunks)
    def _(ch):
        for o in range(n):
            for half in range(halves):
                for i in range(chunk):
                    row = o * rows_own + ch * chunk + i
                    taken = normed.at[half][pl.ds(row, lon_cols, stride=lat_rows), :]
                    stage.at[o % 2, half][pl.ds(i, lon_cols, stride=slot), :] = taken
                xs[o, ch, :, lanes(half)] = stage[o % 2, half].astype(BF16)
        for d in range(n - 1):
            forth(ch, d).start()
        recv[me, ch] = xs[me, ch]

    for weight, turned in ((wqkv1, wqvt1), (wqkv2, wqvt2)):
        turned[:features] = weight[:, :features].astype(F32).T.astype(BF16)
        turned[features:] = weight[:, split:].astype(F32).T.astype(BF16)

    log2e = math.log2(math.e)
    factors1 = [scales[0, h] * log2e for h in range(heads)]
    factors2 = [scales[1, h] * log2e for h in range(heads)]
    at_once = chunk if n * lon_cols <= 256 else 1

    @pl.loop(0, chunks)
    def _(ch):
        for d in range(n - 1):
            forth(ch, d).wait_recv()
        for j in range(n):
            for half in range(halves):
                arrived = recv[j, ch, :, lanes(half)].astype(F32)
                lines[half, j * tokens : (j + 1) * tokens, :] = arrived

        @pl.loop(0, chunk // at_once)
        def _(step):
            taken = []
            for k in range(at_once):
                place = pl.ds(step * at_once + k, n * lon_cols, stride=slot)
                line = [lines.at[half][place, :] for half in range(halves)]
                taken.append(jnp.concatenate(line, 1).astype(BF16))
            result = attend(
                taken, wqkv1[:, features:split], wqvt1[...], wo1[...], factors1, heads
            )
            for k in range(at_once):
                row = ch * chunk + step * at_once + k
                place = pl.ds(row, n * lon_cols, stride=rows_own)
                own = result[k * (n * lon_cols) : (k + 1) * (n * lon_cols)]
                for half in range(halves):
                    mixed.at[half][place, :] = own[:, lanes(half)]

    spare = segment - m * rows_own

    def group(t):
        return lax.rem(t + (cols_own - margin), cols_own)

    @pl.loop(0, cols_own)
    def _(t):
        c = group(t)
        for j in range(n):
            for half in range(halves):
                pieces = []
                for p in range(m):
                    start = (j * lon_cols + p * cols_own + c) * rows_own
                    if rows_own % 8 == 0:
                        start = pl.multiple_of(start, 8)
                    pieces.append(mixed[half, pl.ds(start, rows_own), :])
                if spare:
                    pieces.append(jnp.zeros((spare, LANES), F32))
                block = jnp.concatenate(pieces, 0).astype(BF16)
                obuf[j, c, :, lanes(half)] = block
        for d in range(n - 1):
            back(c, d).start()
        ret[me, c] = obuf[me, c]

    def finish_lon(c):
        for d in range(n - 1):
            back(c, d).wait_recv()
        arrived = [ret[o, c].astype(F32) for o in range(n)]
        for p in range(m):
            lon_mix = jnp.concatenate(
                [block[p * rows_own : (p + 1) * rows_own] for block in arrived], 0
            )
            first = (x_ref[p * cols_own + c].astype(F32) + lon_mix).astype(BF16).astype(F32)
            state[c, p] = first
            lsend[p, c] = layer_norm(first, gains[1:2]).astype(BF16)
        for d in range(m - 1):
            lat_forth(c, d).start()
        lrecv[mine, c] = lsend[mine, c]

    def lat_line(c):
        for d in range(m - 1):
            lat_forth(c, d).wait_recv()
        line = lrecv[:, c].reshape(m * lat_rows, features)
        result = attend(
            [line], wqkv2[:, features:split], wqvt2[...], wo2[...], factors2, heads
        )
        lout[:, c] = result.astype(BF16).reshape(m, lat_rows, features)
        for d in range(m - 1):
            lat_back(c, d).start()
        lret[mine, c] = lout[mine, c]

    def keep_rims(col, block):
        place = pl.ds(pl.multiple_of(col * 8, 8), 8)
        for half in range(halves):
            rims[0, half, place, :] = block[:8, lanes(half)]
            rims[1, half, place, :] = block[lat_rows - 8 :, lanes(half)]

    def finish_lat(c):
        for d in range(m - 1):
            lat_back(c, d).wait_recv()
        for p in range(m):
            total = (state[c, p] + lret[p, c].astype(F32)).astype(BF16)
            col = margin + p * cols_own + c
            out_ref[col] = total
            keep_rims(col, total.astype(F32))

    finish_lon(group(0))

    @pl.loop(0, cols_own)
    def _(t):
        @pl.when(t < cols_own - 1)
        def _():
            finish_lon(group(t + 1))

        lat_line(group(t))

        @pl.when(t > 0)
        def _():
            finish_lat(group(t - 1))

        if cols_own > 2 * margin:

            @pl.when(t == 2 * margin)
            def _():
                for side in range(2):
                    edge(side).start()

    finish_lat(group(cols_own - 1))
    if cols_own <= 2 * margin:
        for side in range(2):
            edge(side).start()

    for side, base in enumerate((0, margin + lon_cols)):
        edge(1 - side).wait_recv()
        for k in range(margin):
            out_ref[base + k] = erecv[side, k]
            keep_rims(base + k, erecv[side, k].astype(F32))

    ends = (mine > 0, mine < m - 1)
    for side, base in enumerate((0, 8 - margin)):
        for k in range(margin):
            for half in range(halves):
                row = rims.at[side, half][pl.ds(base + k, width, stride=8), :]
                hsend[side, k, :, lanes(half)] = row.astype(BF16)

        @pl.when(ends[side])
        def _():
            border(side).start()

    halo_ref[...] = jnp.zeros(halo_ref.shape, F32)
    for side, base in enumerate((8 - margin, 0)):

        @pl.when(ends[side])
        def _():
            border(1 - side).wait_recv()
            for k in range(margin):
                for half in range(halves):
                    row = hrecv[side, k, :, lanes(half)].astype(F32)
                    halo_ref.at[side, half][pl.ds(base + k, width, stride=8), :] = row

    for side in range(2):
        edge(side).wait_send()

        @pl.when(ends[side])
        def _():
            border(side).wait_send()

    @pl.loop(0, chunks)
    def _(ch):
        for d in range(n - 1):
            forth(ch, d).wait_send()

    @pl.loop(0, cols_own)
    def _(c):
        for d in range(n - 1):
            back(c, d).wait_send()
        for d in range(m - 1):
            lat_forth(c, d).wait_send()
            lat_back(c, d).wait_send()


def attention(fields, norm_gains, lon_qkv, lon_out, lat_qkv, lat_out, logit_scales):
    lon_cols, lat_rows, features = fields.shape
    heads = logit_scales.shape[1]
    n, m = lax.axis_size("lon"), lax.axis_size("lat")
    margin = KERNEL // 2
    width = lon_cols + 2 * margin
    rows_own, cols_own = lat_rows // n, lon_cols // m
    chunk = next(size for size in (4, 3, 2, 1) if rows_own % size == 0)
    slot = chunk
    while lon_cols * slot % 16:
        slot += 1
    tokens = lon_cols * slot
    chunks, halves = rows_own // chunk, features // LANES
    segment = -(-(m * rows_own) // 16) * 16
    vmem = pl.BlockSpec(memory_space=pltpu.VMEM)
    dma = pltpu.SemaphoreType.DMA
    groups = (m, cols_own, lat_rows, features)
    return pl.pallas_call(
        functools.partial(attention_kernel, n, m, heads, lon_cols, chunk),
        out_shape=(
            jax.ShapeDtypeStruct((width, lat_rows, features), BF16),
            jax.ShapeDtypeStruct((2, halves, width * 8, LANES), F32),
        ),
        in_specs=[vmem] * 6 + [pl.BlockSpec(memory_space=pltpu.SMEM)],
        out_specs=(vmem, vmem),
        scratch_shapes=[
            pltpu.VMEM((n, chunks, tokens, features), BF16),
            pltpu.VMEM((n, chunks, tokens, features), BF16),
            pltpu.VMEM((halves, lon_cols * lat_rows, LANES), F32),
            pltpu.VMEM((2, halves, tokens, LANES), F32),
            pltpu.VMEM((halves, n * tokens, LANES), F32),
            pltpu.VMEM((halves, n * lon_cols * rows_own, LANES), F32),
            pltpu.VMEM((n, cols_own, segment, features), BF16),
            pltpu.VMEM((n, cols_own, segment, features), BF16),
            pltpu.VMEM((cols_own, m, lat_rows, features), F32),
            pltpu.VMEM(groups, BF16),
            pltpu.VMEM(groups, BF16),
            pltpu.VMEM(groups, BF16),
            pltpu.VMEM(groups, BF16),
            pltpu.VMEM((2 * features, features), BF16),
            pltpu.VMEM((2 * features, features), BF16),
            pltpu.VMEM((2, margin, lat_rows, features), BF16),
            pltpu.VMEM((2, halves, width * 8, LANES), F32),
            pltpu.VMEM((2, margin, width, features), BF16),
            pltpu.VMEM((2, margin, width, features), BF16),
            dma((chunks, n - 1)), dma((chunks, n - 1)),
            dma((cols_own, n - 1)), dma((cols_own, n - 1)),
            dma((cols_own, m - 1)), dma((cols_own, m - 1)),
            dma((cols_own, m - 1)), dma((cols_own, m - 1)),
            dma((2,)), dma((2,)), dma((2,)), dma((2,)),
        ],
        compiler_params=pltpu.CompilerParams(
            collective_id=0, has_side_effects=True, vmem_limit_bytes=60 * 2**20
        ),
    )(fields, norm_gains, lon_qkv, lon_out, lat_qkv, lat_out, logit_scales)


def mixer_kernel(cols, wide, halo, taps, gains, w_in, w_down, out):
    first = pl.program_id(0) * cols
    rows, features = wide.shape[1:]
    hidden_len = w_down.shape[0]
    margin = KERNEL // 2
    count = cols + 2 * margin
    body = wide[pl.ds(first, count)].astype(F32)
    place = pl.ds(pl.multiple_of(first * 8, 8), count * 8)
    rims = [
        jnp.concatenate([halo[side, half, place, :] for half in range(features // LANES)], 1)
        for side in range(2)
    ]
    rims = [rim.reshape(count, 8, features) for rim in rims]
    lines = jnp.concatenate([rims[0], body, rims[1]], 1)
    smoothed = None
    for dy in range(KERNEL):
        term = None
        for dx in range(KERNEL):
            tap = taps[pl.ds(dy * KERNEL + dx, 1), :][None]
            piece = tap * lines[dx : dx + cols]
            term = piece if term is None else term + piece
        term = term[:, 8 - margin + dy : 8 - margin + dy + rows]
        smoothed = term if smoothed is None else smoothed + term
    normed = layer_norm(smoothed.reshape(cols * rows, features), gains[2:3]).astype(BF16)
    gate_up = jnp.dot(normed, w_in[...], preferred_element_type=F32)
    half = gate_up[:, :hidden_len] * 0.5
    hidden = (half * (1.0 + jnp.tanh(half)) * gate_up[:, hidden_len:]).astype(BF16)
    update = jnp.dot(hidden, w_down[...], preferred_element_type=F32)
    total = body[margin : margin + cols] + update.reshape(cols, rows, features)
    out[...] = total.astype(BF16)


def mixer(widened, halo, conv_taps, norm_gains, mlp_in, mlp_down):
    width, lat_rows, features = widened.shape
    lon_cols = width - KERNEL + 1
    cols = next(size for size in (4, 3, 2, 1) if lon_cols % size == 0)
    vmem = pl.BlockSpec(memory_space=pltpu.VMEM)
    return pl.pallas_call(
        functools.partial(mixer_kernel, cols),
        grid=(lon_cols // cols,),
        out_shape=jax.ShapeDtypeStruct((lon_cols, lat_rows, features), BF16),
        in_specs=[vmem] * 6,
        out_specs=pl.BlockSpec((cols, lat_rows, features), lambda i: (i, 0, 0)),
        compiler_params=pltpu.CompilerParams(vmem_limit_bytes=60 * 2**20),
    )(widened, halo, conv_taps, norm_gains, mlp_in, mlp_down)


def per_device(
    fields, norm_gains, lon_qkv, lon_out, lat_qkv, lat_out, logit_scales, conv_taps, mlp_in, mlp_down
):
    columns = jnp.swapaxes(fields, 0, 1)
    widened, halo = attention(
        columns, norm_gains, lon_qkv, lon_out, lat_qkv, lat_out, logit_scales
    )
    return jnp.swapaxes(mixer(widened, halo, conv_taps, norm_gains, mlp_in, mlp_down), 0, 1)


def solution(mesh):
    in_specs = (P(("groups", "lat"), "lon", None), P(), P(), P(), P(), P(), P(), P(), P(), P())
    out_specs = P(("groups", "lat"), "lon", None)
    return jax.shard_map(
        per_device, mesh=mesh, in_specs=in_specs, out_specs=out_specs, check_vma=False
    )
```

```python
import functools
import math

import jax
import jax.numpy as jnp
from jax import lax
from jax.experimental import pallas as pl
from jax.experimental.pallas import tpu as pltpu
from jax.sharding import PartitionSpec as P

KERNEL = 5
LANES = 128
EPSILON = 1e-05
MESH = pl.DeviceIdType.MESH
F32, BF16 = jnp.float32, jnp.bfloat16
NT = (((1,), (1,)), ((), ()))
TN = (((0,), (0,)), ((), ()))


def layer_norm(values, gains):
    average = jnp.mean(values, -1, keepdims=True)
    centred = values - average
    spread = jnp.mean(centred * centred, -1, keepdims=True)
    return centred * lax.rsqrt(spread + EPSILON) * gains


def attend(lines, wk, wqvt, wout, factors, heads):
    length, features = lines[0].shape
    size = features // heads
    together = max(1, min(heads, 5 * 2**20 // (4 * length * length)))
    lane = lax.broadcasted_iota(jnp.int32, (1, features), 1) // size
    masks = [(lane == h).astype(F32).astype(BF16) for h in range(heads)]
    all_keys = jnp.dot(jnp.concatenate(lines, 0), wk, preferred_element_type=F32).astype(BF16)
    contexts = []
    for number, x in enumerate(lines):
        keys = all_keys[number * length : (number + 1) * length]
        qvt = lax.dot_general(wqvt, x, NT, preferred_element_type=F32).astype(BF16)
        queries, values = qvt[:features], qvt[features:]
        parts = []
        for base in range(0, heads, together):
            group = range(base, min(heads, base + together))
            own = jnp.concatenate([keys * masks[h] for h in group], 0)
            scores = jnp.dot(own, queries, preferred_element_type=F32)
            for h in group:
                score = scores[(h - base) * length : (h - base + 1) * length]
                top = jnp.max(score, 0, keepdims=True)
                weights = jnp.exp2((score - top) * factors[h])
                total = jnp.sum(weights, 0, keepdims=True)
                part = jnp.dot(
                    values[h * size : (h + 1) * size],
                    weights.astype(BF16),
                    preferred_element_type=F32,
                )
                parts.append(part * (1.0 / total))
        contexts.append(jnp.concatenate(parts, 0).astype(BF16).T)
    return jnp.dot(jnp.concatenate(contexts, 0), wout, preferred_element_type=F32)


def attention_kernel(
    n, m, heads, lon_cols, chunk,
    x_ref, gains, wqkv1, wo1, wqkv2, wo2, scales,
    out_ref, halo_ref,
    xs, recv, normed, stage, lines, mixed, obuf, ret, state, lsend, lrecv, lout, lret, wqvt1, wqvt2, erecv, rims, hsend, hrecv,
    fs, fr, bs, br, gs, gr, hs, hr, es, er, rs, rr,
):
    lat_rows, features = x_ref.shape[1:]
    rows_own = lat_rows // n
    chunks = rows_own // chunk
    tokens = xs.shape[2]
    slot = tokens // lon_cols
    width = lon_cols + KERNEL - 1
    cols_own = lon_cols // m
    halves = features // LANES
    split = 2 * features
    segment = obuf.shape[2]
    me = lax.axis_index("lon")
    mine = lax.axis_index("lat")
    lon_peers = [lax.rem(me + d, n) for d in range(1, n)]
    lat_peers = [lax.rem(mine + d, m) for d in range(1, m)]

    barrier = pltpu.get_barrier_semaphore()
    for peer in lon_peers:
        pl.semaphore_signal(barrier, inc=1, device_id={"lon": peer}, device_id_type=MESH)
    for peer in lat_peers:
        pl.semaphore_signal(barrier, inc=1, device_id={"lat": peer}, device_id_type=MESH)
    pl.semaphore_wait(barrier, n + m - 2)

    def forth(ch, d):
        peer = lon_peers[d]
        return pltpu.make_async_remote_copy(
            src_ref=xs.at[peer, ch], dst_ref=recv.at[me, ch],
            send_sem=fs.at[ch, d], recv_sem=fr.at[ch, d],
            device_id={"lon": peer}, device_id_type=MESH,
        )

    def back(c, d):
        peer = lon_peers[d]
        return pltpu.make_async_remote_copy(
            src_ref=obuf.at[peer, c], dst_ref=ret.at[me, c],
            send_sem=bs.at[c, d], recv_sem=br.at[c, d],
            device_id={"lon": peer}, device_id_type=MESH,
        )

    def lat_forth(c, d):
        peer = lat_peers[d]
        return pltpu.make_async_remote_copy(
            src_ref=lsend.at[peer, c], dst_ref=lrecv.at[mine, c],
            send_sem=gs.at[c, d], recv_sem=gr.at[c, d],
            device_id={"lat": peer}, device_id_type=MESH,
        )

    def lat_back(c, d):
        peer = lat_peers[d]
        return pltpu.make_async_remote_copy(
            src_ref=lout.at[peer, c], dst_ref=lret.at[mine, c],
            send_sem=hs.at[c, d], recv_sem=hr.at[c, d],
            device_id={"lat": peer}, device_id_type=MESH,
        )

    margin = KERNEL // 2
    left, right = lax.rem(me + n - 1, n), lax.rem(me + 1, n)
    above, below = lax.rem(mine + m - 1, m), lax.rem(mine + 1, m)

    def edge(side):
        start = (margin, lon_cols)[side]
        return pltpu.make_async_remote_copy(
            src_ref=out_ref.at[pl.ds(start, margin)], dst_ref=erecv.at[1 - side],
            send_sem=es.at[side], recv_sem=er.at[1 - side],
            device_id={"lon": (left, right)[side]}, device_id_type=MESH,
        )

    def border(side):
        return pltpu.make_async_remote_copy(
            src_ref=hsend.at[side], dst_ref=hrecv.at[1 - side],
            send_sem=rs.at[side], recv_sem=rr.at[1 - side],
            device_id={"lat": (above, below)[side]}, device_id_type=MESH,
        )

    def lanes(half):
        return slice(half * LANES, (half + 1) * LANES)

    @pl.loop(0, lon_cols)
    def _(col):
        block = layer_norm(x_ref[col].astype(F32), gains[0:1])
        place = pl.ds(pl.multiple_of(col * lat_rows, 8), lat_rows)
        for half in range(halves):
            normed[half, place, :] = block[:, lanes(half)]

    if slot > chunk:
        stage[...] = jnp.zeros(stage.shape, F32)

    @pl.loop(0, chunks)
    def _(ch):
        for o in range(n):
            for half in range(halves):
                for i in range(chunk):
                    row = o * rows_own + ch * chunk + i
                    taken = normed.at[half][pl.ds(row, lon_cols, stride=lat_rows), :]
                    stage.at[o % 2, half][pl.ds(i, lon_cols, stride=slot), :] = taken
                xs[o, ch, :, lanes(half)] = stage[o % 2, half].astype(BF16)
        for d in range(n - 1):
            forth(ch, d).start()
        recv[me, ch] = xs[me, ch]

    for weight, turned in ((wqkv1, wqvt1), (wqkv2, wqvt2)):
        turned[:features] = weight[:, :features].astype(F32).T.astype(BF16)
        turned[features:] = weight[:, split:].astype(F32).T.astype(BF16)

    log2e = math.log2(math.e)
    factors1 = [scales[0, h] * log2e for h in range(heads)]
    factors2 = [scales[1, h] * log2e for h in range(heads)]
    at_once = chunk if n * lon_cols <= 256 else 1

    @pl.loop(0, chunks)
    def _(ch):
        for d in range(n - 1):
            forth(ch, d).wait_recv()
        for j in range(n):
            for half in range(halves):
                arrived = recv[j, ch, :, lanes(half)].astype(F32)
                lines[half, j * tokens : (j + 1) * tokens, :] = arrived

        @pl.loop(0, chunk // at_once)
        def _(step):
            taken = []
            for k in range(at_once):
                place = pl.ds(step * at_once + k, n * lon_cols, stride=slot)
                line = [lines.at[half][place, :] for half in range(halves)]
                taken.append(jnp.concatenate(line, 1).astype(BF16))
            result = attend(
                taken, wqkv1[:, features:split], wqvt1[...], wo1[...], factors1, heads
            )
            for k in range(at_once):
                row = ch * chunk + step * at_once + k
                place = pl.ds(row, n * lon_cols, stride=rows_own)
                own = result[k * (n * lon_cols) : (k + 1) * (n * lon_cols)]
                for half in range(halves):
                    mixed.at[half][place, :] = own[:, lanes(half)]

    spare = segment - m * rows_own

    def group(t):
        return lax.rem(t + (cols_own - margin), cols_own)

    @pl.loop(0, cols_own)
    def _(t):
        c = group(t)
        for j in range(n):
            for half in range(halves):
                pieces = []
                for p in range(m):
                    start = (j * lon_cols + p * cols_own + c) * rows_own
                    if rows_own % 8 == 0:
                        start = pl.multiple_of(start, 8)
                    pieces.append(mixed[half, pl.ds(start, rows_own), :])
                if spare:
                    pieces.append(jnp.zeros((spare, LANES), F32))
                block = jnp.concatenate(pieces, 0).astype(BF16)
                obuf[j, c, :, lanes(half)] = block
        for d in range(n - 1):
            back(c, d).start()
        ret[me, c] = obuf[me, c]

    def finish_lon(c):
        for d in range(n - 1):
            back(c, d).wait_recv()
        arrived = [ret[o, c].astype(F32) for o in range(n)]
        for p in range(m):
            lon_mix = jnp.concatenate(
                [block[p * rows_own : (p + 1) * rows_own] for block in arrived], 0
            )
            first = (x_ref[p * cols_own + c].astype(F32) + lon_mix).astype(BF16).astype(F32)
            state[c, p] = first
            lsend[p, c] = layer_norm(first, gains[1:2]).astype(BF16)
        for d in range(m - 1):
            lat_forth(c, d).start()
        lrecv[mine, c] = lsend[mine, c]

    def lat_line(c):
        for d in range(m - 1):
            lat_forth(c, d).wait_recv()
        line = lrecv[:, c].reshape(m * lat_rows, features)
        result = attend(
            [line], wqkv2[:, features:split], wqvt2[...], wo2[...], factors2, heads
        )
        lout[:, c] = result.astype(BF16).reshape(m, lat_rows, features)
        for d in range(m - 1):
            lat_back(c, d).start()
        lret[mine, c] = lout[mine, c]

    def keep_rims(col, block):
        place = pl.ds(pl.multiple_of(col * 8, 8), 8)
        for half in range(halves):
            rims[0, half, place, :] = block[:8, lanes(half)]
            rims[1, half, place, :] = block[lat_rows - 8 :, lanes(half)]

    def finish_lat(c):
        for d in range(m - 1):
            lat_back(c, d).wait_recv()
        for p in range(m):
            total = (state[c, p] + lret[p, c].astype(F32)).astype(BF16)
            col = margin + p * cols_own + c
            out_ref[col] = total
            keep_rims(col, total.astype(F32))

    finish_lon(group(0))

    @pl.loop(0, cols_own)
    def _(t):
        @pl.when(t < cols_own - 1)
        def _():
            finish_lon(group(t + 1))

        lat_line(group(t))

        @pl.when(t > 0)
        def _():
            finish_lat(group(t - 1))

        if cols_own > 2 * margin:

            @pl.when(t == 2 * margin)
            def _():
                for side in range(2):
                    edge(side).start()

    finish_lat(group(cols_own - 1))
    if cols_own <= 2 * margin:
        for side in range(2):
            edge(side).start()

    for side, base in enumerate((0, margin + lon_cols)):
        edge(1 - side).wait_recv()
        for k in range(margin):
            out_ref[base + k] = erecv[side, k]
            keep_rims(base + k, erecv[side, k].astype(F32))

    ends = (mine > 0, mine < m - 1)
    for side, base in enumerate((0, 8 - margin)):
        for k in range(margin):
            for half in range(halves):
                row = rims.at[side, half][pl.ds(base + k, width, stride=8), :]
                hsend[side, k, :, lanes(half)] = row.astype(BF16)

        @pl.when(ends[side])
        def _():
            border(side).start()

    halo_ref[...] = jnp.zeros(halo_ref.shape, F32)
    for side, base in enumerate((8 - margin, 0)):

        @pl.when(ends[side])
        def _():
            border(1 - side).wait_recv()
            for k in range(margin):
                for half in range(halves):
                    row = hrecv[side, k, :, lanes(half)].astype(F32)
                    halo_ref.at[side, half][pl.ds(base + k, width, stride=8), :] = row

    for side in range(2):
        edge(side).wait_send()

        @pl.when(ends[side])
        def _():
            border(side).wait_send()

    @pl.loop(0, chunks)
    def _(ch):
        for d in range(n - 1):
            forth(ch, d).wait_send()

    @pl.loop(0, cols_own)
    def _(c):
        for d in range(n - 1):
            back(c, d).wait_send()
        for d in range(m - 1):
            lat_forth(c, d).wait_send()
            lat_back(c, d).wait_send()


def attention(fields, norm_gains, lon_qkv, lon_out, lat_qkv, lat_out, logit_scales):
    lon_cols, lat_rows, features = fields.shape
    heads = logit_scales.shape[1]
    n, m = lax.axis_size("lon"), lax.axis_size("lat")
    margin = KERNEL // 2
    width = lon_cols + 2 * margin
    rows_own, cols_own = lat_rows // n, lon_cols // m
    chunk = next(size for size in (4, 3, 2, 1) if rows_own % size == 0)
    slot = chunk
    while lon_cols * slot % 16:
        slot += 1
    tokens = lon_cols * slot
    chunks, halves = rows_own // chunk, features // LANES
    segment = -(-(m * rows_own) // 16) * 16
    vmem = pl.BlockSpec(memory_space=pltpu.VMEM)
    dma = pltpu.SemaphoreType.DMA
    groups = (m, cols_own, lat_rows, features)
    return pl.pallas_call(
        functools.partial(attention_kernel, n, m, heads, lon_cols, chunk),
        out_shape=(
            jax.ShapeDtypeStruct((width, lat_rows, features), BF16),
            jax.ShapeDtypeStruct((2, halves, width * 8, LANES), F32),
        ),
        in_specs=[vmem] * 6 + [pl.BlockSpec(memory_space=pltpu.SMEM)],
        out_specs=(vmem, vmem),
        scratch_shapes=[
            pltpu.VMEM((n, chunks, tokens, features), BF16),
            pltpu.VMEM((n, chunks, tokens, features), BF16),
            pltpu.VMEM((halves, lon_cols * lat_rows, LANES), F32),
            pltpu.VMEM((2, halves, tokens, LANES), F32),
            pltpu.VMEM((halves, n * tokens, LANES), F32),
            pltpu.VMEM((halves, n * lon_cols * rows_own, LANES), F32),
            pltpu.VMEM((n, cols_own, segment, features), BF16),
            pltpu.VMEM((n, cols_own, segment, features), BF16),
            pltpu.VMEM((cols_own, m, lat_rows, features), F32),
            pltpu.VMEM(groups, BF16),
            pltpu.VMEM(groups, BF16),
            pltpu.VMEM(groups, BF16),
            pltpu.VMEM(groups, BF16),
            pltpu.VMEM((2 * features, features), BF16),
            pltpu.VMEM((2 * features, features), BF16),
            pltpu.VMEM((2, margin, lat_rows, features), BF16),
            pltpu.VMEM((2, halves, width * 8, LANES), F32),
            pltpu.VMEM((2, margin, width, features), BF16),
            pltpu.VMEM((2, margin, width, features), BF16),
            dma((chunks, n - 1)), dma((chunks, n - 1)),
            dma((cols_own, n - 1)), dma((cols_own, n - 1)),
            dma((cols_own, m - 1)), dma((cols_own, m - 1)),
            dma((cols_own, m - 1)), dma((cols_own, m - 1)),
            dma((2,)), dma((2,)), dma((2,)), dma((2,)),
        ],
        compiler_params=pltpu.CompilerParams(
            collective_id=0, has_side_effects=True, vmem_limit_bytes=60 * 2**20
        ),
    )(fields, norm_gains, lon_qkv, lon_out, lat_qkv, lat_out, logit_scales)


def mixer_kernel(cols, wide, halo, taps, gains, w_in, w_down, out):
    first = pl.program_id(0) * cols
    rows, features = wide.shape[1:]
    hidden_len = w_down.shape[0]
    margin = KERNEL // 2
    count = cols + 2 * margin
    body = wide[pl.ds(first, count)].astype(F32)
    place = pl.ds(pl.multiple_of(first * 8, 8), count * 8)
    rims = [
        jnp.concatenate([halo[side, half, place, :] for half in range(features // LANES)], 1)
        for side in range(2)
    ]
    rims = [rim.reshape(count, 8, features) for rim in rims]
    lines = jnp.concatenate([rims[0], body, rims[1]], 1)
    smoothed = None
    for dy in range(KERNEL):
        term = None
        for dx in range(KERNEL):
            tap = taps[pl.ds(dy * KERNEL + dx, 1), :][None]
            piece = tap * lines[dx : dx + cols]
            term = piece if term is None else term + piece
        term = term[:, 8 - margin + dy : 8 - margin + dy + rows]
        smoothed = term if smoothed is None else smoothed + term
    normed = layer_norm(smoothed.reshape(cols * rows, features), gains[2:3]).astype(BF16)
    step = min(hidden_len, 256)
    update = None
    for base in range(0, hidden_len, step):
        gate = jnp.dot(normed, w_in[:, base : base + step], preferred_element_type=F32)
        up = jnp.dot(
            normed, w_in[:, hidden_len + base : hidden_len + base + step], preferred_element_type=F32
        )
        half = gate * 0.5
        hidden = (half * (1.0 + jnp.tanh(half)) * up).astype(BF16)
        share = jnp.dot(hidden, w_down[base : base + step, :], preferred_element_type=F32)
        update = share if update is None else update + share
    total = body[margin : margin + cols] + update.reshape(cols, rows, features)
    out[...] = total.astype(BF16)


def mixer(widened, halo, conv_taps, norm_gains, mlp_in, mlp_down):
    width, lat_rows, features = widened.shape
    lon_cols = width - KERNEL + 1
    cols = next(size for size in (7, 6, 5, 4, 3, 2, 1) if lon_cols % size == 0)
    vmem = pl.BlockSpec(memory_space=pltpu.VMEM)
    return pl.pallas_call(
        functools.partial(mixer_kernel, cols),
        grid=(lon_cols // cols,),
        out_shape=jax.ShapeDtypeStruct((lon_cols, lat_rows, features), BF16),
        in_specs=[vmem] * 6,
        out_specs=pl.BlockSpec((cols, lat_rows, features), lambda i: (i, 0, 0)),
        compiler_params=pltpu.CompilerParams(vmem_limit_bytes=60 * 2**20),
    )(widened, halo, conv_taps, norm_gains, mlp_in, mlp_down)


def per_device(
    fields, norm_gains, lon_qkv, lon_out, lat_qkv, lat_out, logit_scales, conv_taps, mlp_in, mlp_down
):
    columns = jnp.swapaxes(fields, 0, 1)
    widened, halo = attention(
        columns, norm_gains, lon_qkv, lon_out, lat_qkv, lat_out, logit_scales
    )
    return jnp.swapaxes(mixer(widened, halo, conv_taps, norm_gains, mlp_in, mlp_down), 0, 1)


def solution(mesh):
    in_specs = (P(("groups", "lat"), "lon", None), P(), P(), P(), P(), P(), P(), P(), P(), P())
    out_specs = P(("groups", "lat"), "lon", None)
    return jax.shard_map(
        per_device, mesh=mesh, in_specs=in_specs, out_specs=out_specs, check_vma=False
    )
```

```python
import functools
import math

import jax
import jax.numpy as jnp
from jax import lax
from jax.experimental import pallas as pl
from jax.experimental.pallas import tpu as pltpu
from jax.sharding import PartitionSpec as P

KERNEL = 5
LANES = 128
EPSILON = 1e-05
MESH = pl.DeviceIdType.MESH
F32, BF16 = jnp.float32, jnp.bfloat16
NT = (((1,), (1,)), ((), ()))
TN = (((0,), (0,)), ((), ()))


def layer_norm(values, gains):
    average = jnp.mean(values, -1, keepdims=True)
    centred = values - average
    spread = jnp.mean(centred * centred, -1, keepdims=True)
    return centred * lax.rsqrt(spread + EPSILON) * gains


def attend(lines, wk, wqvt, wout, factors, heads):
    length, features = lines[0].shape
    size = features // heads
    together = max(1, min(heads, 5 * 2**20 // (4 * length * length)))
    lane = lax.broadcasted_iota(jnp.int32, (1, features), 1) // size
    masks = [(lane == h).astype(F32).astype(BF16) for h in range(heads)]
    all_keys = jnp.dot(jnp.concatenate(lines, 0), wk, preferred_element_type=F32).astype(BF16)
    contexts = []
    for number, x in enumerate(lines):
        keys = all_keys[number * length : (number + 1) * length]
        qvt = lax.dot_general(wqvt, x, NT, preferred_element_type=F32).astype(BF16)
        queries, values = qvt[:features], qvt[features:]
        parts = []
        for base in range(0, heads, together):
            group = range(base, min(heads, base + together))
            own = jnp.concatenate([keys * masks[h] for h in group], 0)
            scores = jnp.dot(own, queries, preferred_element_type=F32)
            for h in group:
                score = scores[(h - base) * length : (h - base + 1) * length]
                top = jnp.max(score, 0, keepdims=True)
                weights = jnp.exp2((score - top) * factors[h])
                total = jnp.sum(weights, 0, keepdims=True)
                part = jnp.dot(
                    values[h * size : (h + 1) * size],
                    weights.astype(BF16),
                    preferred_element_type=F32,
                )
                parts.append(part * (1.0 / total))
        contexts.append(jnp.concatenate(parts, 0).astype(BF16).T)
    return jnp.dot(jnp.concatenate(contexts, 0), wout, preferred_element_type=F32)


def attention_kernel(
    n, m, heads, lon_cols, chunk,
    x_ref, gains, wqkv1, wo1, wqkv2, wo2, scales,
    out_ref, halo_ref,
    xs, recv, normed, stage, lines, mixed, obuf, ret, state, lsend, lrecv, lout, lret, wqvt1, wqvt2, erecv, rims, hsend, hrecv,
    fs, fr, bs, br, gs, gr, hs, hr, es, er, rs, rr,
):
    lat_rows, features = x_ref.shape[1:]
    rows_own = lat_rows // n
    chunks = rows_own // chunk
    tokens = xs.shape[2]
    slot = tokens // lon_cols
    width = lon_cols + KERNEL - 1
    cols_own = lon_cols // m
    halves = features // LANES
    split = 2 * features
    segment = obuf.shape[2]
    me = lax.axis_index("lon")
    mine = lax.axis_index("lat")
    lon_peers = [lax.rem(me + d, n) for d in range(1, n)]
    lat_peers = [lax.rem(mine + d, m) for d in range(1, m)]

    barrier = pltpu.get_barrier_semaphore()
    for peer in lon_peers:
        pl.semaphore_signal(barrier, inc=1, device_id={"lon": peer}, device_id_type=MESH)
    for peer in lat_peers:
        pl.semaphore_signal(barrier, inc=1, device_id={"lat": peer}, device_id_type=MESH)
    pl.semaphore_wait(barrier, n + m - 2)

    def forth(ch, d):
        peer = lon_peers[d]
        return pltpu.make_async_remote_copy(
            src_ref=xs.at[peer, ch], dst_ref=recv.at[me, ch],
            send_sem=fs.at[ch, d], recv_sem=fr.at[ch, d],
            device_id={"lon": peer}, device_id_type=MESH,
        )

    def back(c, d):
        peer = lon_peers[d]
        return pltpu.make_async_remote_copy(
            src_ref=obuf.at[peer, c], dst_ref=ret.at[me, c],
            send_sem=bs.at[c, d], recv_sem=br.at[c, d],
            device_id={"lon": peer}, device_id_type=MESH,
        )

    def lat_forth(c, d):
        peer = lat_peers[d]
        return pltpu.make_async_remote_copy(
            src_ref=lsend.at[peer, c], dst_ref=lrecv.at[mine, c],
            send_sem=gs.at[c, d], recv_sem=gr.at[c, d],
            device_id={"lat": peer}, device_id_type=MESH,
        )

    def lat_back(c, d):
        peer = lat_peers[d]
        return pltpu.make_async_remote_copy(
            src_ref=lout.at[peer, c], dst_ref=lret.at[mine, c],
            send_sem=hs.at[c, d], recv_sem=hr.at[c, d],
            device_id={"lat": peer}, device_id_type=MESH,
        )

    margin = KERNEL // 2
    left, right = lax.rem(me + n - 1, n), lax.rem(me + 1, n)
    above, below = lax.rem(mine + m - 1, m), lax.rem(mine + 1, m)

    def edge(side):
        start = (margin, lon_cols)[side]
        return pltpu.make_async_remote_copy(
            src_ref=out_ref.at[pl.ds(start, margin)], dst_ref=erecv.at[1 - side],
            send_sem=es.at[side], recv_sem=er.at[1 - side],
            device_id={"lon": (left, right)[side]}, device_id_type=MESH,
        )

    def border(side):
        return pltpu.make_async_remote_copy(
            src_ref=hsend.at[side], dst_ref=hrecv.at[1 - side],
            send_sem=rs.at[side], recv_sem=rr.at[1 - side],
            device_id={"lat": (above, below)[side]}, device_id_type=MESH,
        )

    def lanes(half):
        return slice(half * LANES, (half + 1) * LANES)

    several = next(size for size in (4, 3, 2, 1) if lon_cols % size == 0)

    @pl.loop(0, lon_cols // several)
    def _(i):
        block = x_ref[pl.ds(i * several, several)].astype(F32)
        block = layer_norm(block.reshape(several * lat_rows, features), gains[0:1])
        place = pl.ds(pl.multiple_of(i * (several * lat_rows), 8), several * lat_rows)
        for half in range(halves):
            normed[half, place, :] = block[:, lanes(half)]

    if slot > chunk:
        stage[...] = jnp.zeros(stage.shape, F32)

    @pl.loop(0, chunks)
    def _(ch):
        for o in range(n):
            for half in range(halves):
                for i in range(chunk):
                    row = o * rows_own + ch * chunk + i
                    taken = normed.at[half][pl.ds(row, lon_cols, stride=lat_rows), :]
                    stage.at[o % 2, half][pl.ds(i, lon_cols, stride=slot), :] = taken
                xs[o, ch, :, lanes(half)] = stage[o % 2, half].astype(BF16)
        for d in range(n - 1):
            forth(ch, d).start()
        recv[me, ch] = xs[me, ch]

    for weight, turned in ((wqkv1, wqvt1), (wqkv2, wqvt2)):
        turned[:features] = weight[:, :features].astype(F32).T.astype(BF16)
        turned[features:] = weight[:, split:].astype(F32).T.astype(BF16)

    log2e = math.log2(math.e)
    factors1 = [scales[0, h] * log2e for h in range(heads)]
    factors2 = [scales[1, h] * log2e for h in range(heads)]
    at_once = chunk if n * lon_cols <= 256 else 1

    @pl.loop(0, chunks)
    def _(ch):
        for d in range(n - 1):
            forth(ch, d).wait_recv()
        for j in range(n):
            for half in range(halves):
                arrived = recv[j, ch, :, lanes(half)].astype(F32)
                lines[half, j * tokens : (j + 1) * tokens, :] = arrived

        @pl.loop(0, chunk // at_once)
        def _(step):
            taken = []
            for k in range(at_once):
                place = pl.ds(step * at_once + k, n * lon_cols, stride=slot)
                line = [lines.at[half][place, :] for half in range(halves)]
                taken.append(jnp.concatenate(line, 1).astype(BF16))
            result = attend(
                taken, wqkv1[:, features:split], wqvt1[...], wo1[...], factors1, heads
            )
            for k in range(at_once):
                row = ch * chunk + step * at_once + k
                place = pl.ds(row, n * lon_cols, stride=rows_own)
                own = result[k * (n * lon_cols) : (k + 1) * (n * lon_cols)]
                for half in range(halves):
                    mixed.at[half][place, :] = own[:, lanes(half)]

    spare = segment - m * rows_own

    def group(t):
        return lax.rem(t + (cols_own - margin), cols_own)

    @pl.loop(0, cols_own)
    def _(t):
        c = group(t)
        for j in range(n):
            for half in range(halves):
                pieces = []
                for p in range(m):
                    start = (j * lon_cols + p * cols_own + c) * rows_own
                    if rows_own % 8 == 0:
                        start = pl.multiple_of(start, 8)
                    pieces.append(mixed[half, pl.ds(start, rows_own), :])
                if spare:
                    pieces.append(jnp.zeros((spare, LANES), F32))
                block = jnp.concatenate(pieces, 0).astype(BF16)
                obuf[j, c, :, lanes(half)] = block
        for d in range(n - 1):
            back(c, d).start()
        ret[me, c] = obuf[me, c]

    def finish_lon(c):
        for d in range(n - 1):
            back(c, d).wait_recv()
        arrived = [ret[o, c].astype(F32) for o in range(n)]
        for p in range(m):
            lon_mix = jnp.concatenate(
                [block[p * rows_own : (p + 1) * rows_own] for block in arrived], 0
            )
            first = (x_ref[p * cols_own + c].astype(F32) + lon_mix).astype(BF16).astype(F32)
            state[c, p] = first
            lsend[p, c] = layer_norm(first, gains[1:2]).astype(BF16)
        for d in range(m - 1):
            lat_forth(c, d).start()
        lrecv[mine, c] = lsend[mine, c]

    def lat_line(c):
        for d in range(m - 1):
            lat_forth(c, d).wait_recv()
        line = lrecv[:, c].reshape(m * lat_rows, features)
        result = attend(
            [line], wqkv2[:, features:split], wqvt2[...], wo2[...], factors2, heads
        )
        lout[:, c] = result.astype(BF16).reshape(m, lat_rows, features)
        for d in range(m - 1):
            lat_back(c, d).start()
        lret[mine, c] = lout[mine, c]

    def keep_rims(col, block):
        place = pl.ds(pl.multiple_of(col * 8, 8), 8)
        for half in range(halves):
            rims[0, half, place, :] = block[:8, lanes(half)]
            rims[1, half, place, :] = block[lat_rows - 8 :, lanes(half)]

    def finish_lat(c):
        for d in range(m - 1):
            lat_back(c, d).wait_recv()
        for p in range(m):
            total = (state[c, p] + lret[p, c].astype(F32)).astype(BF16)
            col = margin + p * cols_own + c
            out_ref[col] = total
            keep_rims(col, total.astype(F32))

    finish_lon(group(0))

    @pl.loop(0, cols_own)
    def _(t):
        @pl.when(t < cols_own - 1)
        def _():
            finish_lon(group(t + 1))

        lat_line(group(t))

        @pl.when(t > 0)
        def _():
            finish_lat(group(t - 1))

        if cols_own > 2 * margin:

            @pl.when(t == 2 * margin)
            def _():
                for side in range(2):
                    edge(side).start()

    finish_lat(group(cols_own - 1))
    if cols_own <= 2 * margin:
        for side in range(2):
            edge(side).start()

    for side, base in enumerate((0, margin + lon_cols)):
        edge(1 - side).wait_recv()
        for k in range(margin):
            out_ref[base + k] = erecv[side, k]
            keep_rims(base + k, erecv[side, k].astype(F32))

    ends = (mine > 0, mine < m - 1)
    for side, base in enumerate((0, 8 - margin)):
        for k in range(margin):
            for half in range(halves):
                row = rims.at[side, half][pl.ds(base + k, width, stride=8), :]
                hsend[side, k, :, lanes(half)] = row.astype(BF16)

        @pl.when(ends[side])
        def _():
            border(side).start()

    halo_ref[...] = jnp.zeros(halo_ref.shape, F32)
    for side, base in enumerate((8 - margin, 0)):

        @pl.when(ends[side])
        def _():
            border(1 - side).wait_recv()
            for k in range(margin):
                for half in range(halves):
                    row = hrecv[side, k, :, lanes(half)].astype(F32)
                    halo_ref.at[side, half][pl.ds(base + k, width, stride=8), :] = row

    for side in range(2):
        edge(side).wait_send()

        @pl.when(ends[side])
        def _():
            border(side).wait_send()

    @pl.loop(0, chunks)
    def _(ch):
        for d in range(n - 1):
            forth(ch, d).wait_send()

    @pl.loop(0, cols_own)
    def _(c):
        for d in range(n - 1):
            back(c, d).wait_send()
        for d in range(m - 1):
            lat_forth(c, d).wait_send()
            lat_back(c, d).wait_send()


def attention(fields, norm_gains, lon_qkv, lon_out, lat_qkv, lat_out, logit_scales):
    lon_cols, lat_rows, features = fields.shape
    heads = logit_scales.shape[1]
    n, m = lax.axis_size("lon"), lax.axis_size("lat")
    margin = KERNEL // 2
    width = lon_cols + 2 * margin
    rows_own, cols_own = lat_rows // n, lon_cols // m
    chunk = next(size for size in (4, 3, 2, 1) if rows_own % size == 0)
    slot = chunk
    while lon_cols * slot % 16:
        slot += 1
    tokens = lon_cols * slot
    chunks, halves = rows_own // chunk, features // LANES
    segment = -(-(m * rows_own) // 16) * 16
    vmem = pl.BlockSpec(memory_space=pltpu.VMEM)
    dma = pltpu.SemaphoreType.DMA
    groups = (m, cols_own, lat_rows, features)
    return pl.pallas_call(
        functools.partial(attention_kernel, n, m, heads, lon_cols, chunk),
        out_shape=(
            jax.ShapeDtypeStruct((width, lat_rows, features), BF16),
            jax.ShapeDtypeStruct((2, halves, width * 8, LANES), F32),
        ),
        in_specs=[vmem] * 6 + [pl.BlockSpec(memory_space=pltpu.SMEM)],
        out_specs=(vmem, vmem),
        scratch_shapes=[
            pltpu.VMEM((n, chunks, tokens, features), BF16),
            pltpu.VMEM((n, chunks, tokens, features), BF16),
            pltpu.VMEM((halves, lon_cols * lat_rows, LANES), F32),
            pltpu.VMEM((2, halves, tokens, LANES), F32),
            pltpu.VMEM((halves, n * tokens, LANES), F32),
            pltpu.VMEM((halves, n * lon_cols * rows_own, LANES), F32),
            pltpu.VMEM((n, cols_own, segment, features), BF16),
            pltpu.VMEM((n, cols_own, segment, features), BF16),
            pltpu.VMEM((cols_own, m, lat_rows, features), F32),
            pltpu.VMEM(groups, BF16),
            pltpu.VMEM(groups, BF16),
            pltpu.VMEM(groups, BF16),
            pltpu.VMEM(groups, BF16),
            pltpu.VMEM((2 * features, features), BF16),
            pltpu.VMEM((2 * features, features), BF16),
            pltpu.VMEM((2, margin, lat_rows, features), BF16),
            pltpu.VMEM((2, halves, width * 8, LANES), F32),
            pltpu.VMEM((2, margin, width, features), BF16),
            pltpu.VMEM((2, margin, width, features), BF16),
            dma((chunks, n - 1)), dma((chunks, n - 1)),
            dma((cols_own, n - 1)), dma((cols_own, n - 1)),
            dma((cols_own, m - 1)), dma((cols_own, m - 1)),
            dma((cols_own, m - 1)), dma((cols_own, m - 1)),
            dma((2,)), dma((2,)), dma((2,)), dma((2,)),
        ],
        compiler_params=pltpu.CompilerParams(
            collective_id=0, has_side_effects=True, vmem_limit_bytes=60 * 2**20
        ),
    )(fields, norm_gains, lon_qkv, lon_out, lat_qkv, lat_out, logit_scales)


def mixer_kernel(cols, wide, halo, taps, gains, w_in, w_down, out):
    first = pl.program_id(0) * cols
    rows, features = wide.shape[1:]
    hidden_len = w_down.shape[0]
    margin = KERNEL // 2
    count = cols + 2 * margin
    body = wide[pl.ds(first, count)].astype(F32)
    place = pl.ds(pl.multiple_of(first * 8, 8), count * 8)
    rims = [
        jnp.concatenate([halo[side, half, place, :] for half in range(features // LANES)], 1)
        for side in range(2)
    ]
    rims = [rim.reshape(count, 8, features) for rim in rims]
    lines = jnp.concatenate([rims[0], body, rims[1]], 1)
    smoothed = None
    for dy in range(KERNEL):
        term = None
        for dx in range(KERNEL):
            tap = taps[pl.ds(dy * KERNEL + dx, 1), :][None]
            piece = tap * lines[dx : dx + cols]
            term = piece if term is None else term + piece
        term = term[:, 8 - margin + dy : 8 - margin + dy + rows]
        smoothed = term if smoothed is None else smoothed + term
    normed = layer_norm(smoothed.reshape(cols * rows, features), gains[2:3]).astype(BF16)
    step = min(hidden_len, 256)
    update = None
    for base in range(0, hidden_len, step):
        gate = jnp.dot(normed, w_in[:, base : base + step], preferred_element_type=F32)
        up = jnp.dot(
            normed, w_in[:, hidden_len + base : hidden_len + base + step], preferred_element_type=F32
        )
        half = gate * 0.5
        hidden = (half * (1.0 + jnp.tanh(half)) * up).astype(BF16)
        share = jnp.dot(hidden, w_down[base : base + step, :], preferred_element_type=F32)
        update = share if update is None else update + share
    total = body[margin : margin + cols] + update.reshape(cols, rows, features)
    out[...] = total.astype(BF16)


def mixer(widened, halo, conv_taps, norm_gains, mlp_in, mlp_down):
    width, lat_rows, features = widened.shape
    lon_cols = width - KERNEL + 1
    cols = next(size for size in (7, 6, 5, 4, 3, 2, 1) if lon_cols % size == 0)
    vmem = pl.BlockSpec(memory_space=pltpu.VMEM)
    return pl.pallas_call(
        functools.partial(mixer_kernel, cols),
        grid=(lon_cols // cols,),
        out_shape=jax.ShapeDtypeStruct((lon_cols, lat_rows, features), BF16),
        in_specs=[vmem] * 6,
        out_specs=pl.BlockSpec((cols, lat_rows, features), lambda i: (i, 0, 0)),
        compiler_params=pltpu.CompilerParams(vmem_limit_bytes=60 * 2**20),
    )(widened, halo, conv_taps, norm_gains, mlp_in, mlp_down)


def per_device(
    fields, norm_gains, lon_qkv, lon_out, lat_qkv, lat_out, logit_scales, conv_taps, mlp_in, mlp_down
):
    columns = jnp.swapaxes(fields, 0, 1)
    widened, halo = attention(
        columns, norm_gains, lon_qkv, lon_out, lat_qkv, lat_out, logit_scales
    )
    return jnp.swapaxes(mixer(widened, halo, conv_taps, norm_gains, mlp_in, mlp_down), 0, 1)


def solution(mesh):
    in_specs = (P(("groups", "lat"), "lon", None), P(), P(), P(), P(), P(), P(), P(), P(), P())
    out_specs = P(("groups", "lat"), "lon", None)
    return jax.shard_map(
        per_device, mesh=mesh, in_specs=in_specs, out_specs=out_specs, check_vma=False
    )
```

```python
import functools
import math

import jax
import jax.numpy as jnp
from jax import lax
from jax.experimental import pallas as pl
from jax.experimental.pallas import tpu as pltpu
from jax.sharding import PartitionSpec as P

KERNEL = 5
LANES = 128
EPSILON = 1e-05
MESH = pl.DeviceIdType.MESH
F32, BF16 = jnp.float32, jnp.bfloat16
NT = (((1,), (1,)), ((), ()))
TN = (((0,), (0,)), ((), ()))


def layer_norm(values, gains):
    average = jnp.mean(values, -1, keepdims=True)
    centred = values - average
    spread = jnp.mean(centred * centred, -1, keepdims=True)
    return centred * lax.rsqrt(spread + EPSILON) * gains


def attend(lines, wk, wqvt, wout, factors, heads):
    length, features = lines[0].shape
    size = features // heads
    together = max(1, min(heads, 5 * 2**20 // (4 * length * length)))
    lane = lax.broadcasted_iota(jnp.int32, (1, features), 1) // size
    masks = [(lane == h).astype(F32).astype(BF16) for h in range(heads)]
    all_keys = jnp.dot(jnp.concatenate(lines, 0), wk, preferred_element_type=F32).astype(BF16)
    contexts = []
    for number, x in enumerate(lines):
        keys = all_keys[number * length : (number + 1) * length]
        qvt = lax.dot_general(wqvt, x, NT, preferred_element_type=F32).astype(BF16)
        queries, values = qvt[:features], qvt[features:]
        parts = []
        for base in range(0, heads, together):
            group = range(base, min(heads, base + together))
            own = jnp.concatenate([keys * masks[h] for h in group], 0)
            scores = jnp.dot(own, queries, preferred_element_type=F32)
            for h in group:
                score = scores[(h - base) * length : (h - base + 1) * length]
                top = jnp.max(score, 0, keepdims=True)
                weights = jnp.exp2((score - top) * factors[h])
                total = jnp.sum(weights, 0, keepdims=True)
                part = jnp.dot(
                    values[h * size : (h + 1) * size],
                    weights.astype(BF16),
                    preferred_element_type=F32,
                )
                parts.append(part * (1.0 / total))
        contexts.append(jnp.concatenate(parts, 0).astype(BF16).T)
    return jnp.dot(jnp.concatenate(contexts, 0), wout, preferred_element_type=F32)


def attention_kernel(
    n, m, heads, lon_cols, chunk,
    x_ref, gains, wqkv1, wo1, wqkv2, wo2, scales,
    out_ref, halo_ref,
    xs, recv, normed, stage, lines, mixed, obuf, ret, state, lsend, lrecv, lout, lret, wqvt1, wqvt2, erecv, rims, hsend, hrecv,
    fs, fr, bs, br, gs, gr, hs, hr, es, er, rs, rr,
):
    lat_rows, features = x_ref.shape[1:]
    rows_own = lat_rows // n
    chunks = rows_own // chunk
    tokens = xs.shape[2]
    slot = tokens // lon_cols
    width = lon_cols + KERNEL - 1
    cols_own = lon_cols // m
    halves = features // LANES
    split = 2 * features
    segment = obuf.shape[2]
    me = lax.axis_index("lon")
    mine = lax.axis_index("lat")
    lon_peers = [lax.rem(me + d, n) for d in range(1, n)]
    lat_peers = [lax.rem(mine + d, m) for d in range(1, m)]

    barrier = pltpu.get_barrier_semaphore()
    for peer in lon_peers:
        pl.semaphore_signal(barrier, inc=1, device_id={"lon": peer}, device_id_type=MESH)
    for peer in lat_peers:
        pl.semaphore_signal(barrier, inc=1, device_id={"lat": peer}, device_id_type=MESH)
    pl.semaphore_wait(barrier, n + m - 2)

    def forth(ch, d):
        peer = lon_peers[d]
        return pltpu.make_async_remote_copy(
            src_ref=xs.at[peer, ch], dst_ref=recv.at[me, ch],
            send_sem=fs.at[ch, d], recv_sem=fr.at[ch, d],
            device_id={"lon": peer}, device_id_type=MESH,
        )

    def back(c, d):
        peer = lon_peers[d]
        return pltpu.make_async_remote_copy(
            src_ref=obuf.at[peer, c], dst_ref=ret.at[me, c],
            send_sem=bs.at[c, d], recv_sem=br.at[c, d],
            device_id={"lon": peer}, device_id_type=MESH,
        )

    def lat_forth(c, d):
        peer = lat_peers[d]
        return pltpu.make_async_remote_copy(
            src_ref=lsend.at[peer, c], dst_ref=lrecv.at[mine, c],
            send_sem=gs.at[c, d], recv_sem=gr.at[c, d],
            device_id={"lat": peer}, device_id_type=MESH,
        )

    def lat_back(c, d):
        peer = lat_peers[d]
        return pltpu.make_async_remote_copy(
            src_ref=lout.at[peer, c], dst_ref=lret.at[mine, c],
            send_sem=hs.at[c, d], recv_sem=hr.at[c, d],
            device_id={"lat": peer}, device_id_type=MESH,
        )

    margin = KERNEL // 2
    left, right = lax.rem(me + n - 1, n), lax.rem(me + 1, n)
    above, below = lax.rem(mine + m - 1, m), lax.rem(mine + 1, m)

    def edge(side):
        start = (margin, lon_cols)[side]
        return pltpu.make_async_remote_copy(
            src_ref=out_ref.at[pl.ds(start, margin)], dst_ref=erecv.at[1 - side],
            send_sem=es.at[side], recv_sem=er.at[1 - side],
            device_id={"lon": (left, right)[side]}, device_id_type=MESH,
        )

    def border(side):
        return pltpu.make_async_remote_copy(
            src_ref=hsend.at[side], dst_ref=hrecv.at[1 - side],
            send_sem=rs.at[side], recv_sem=rr.at[1 - side],
            device_id={"lat": (above, below)[side]}, device_id_type=MESH,
        )

    def lanes(half):
        return slice(half * LANES, (half + 1) * LANES)

    several = next(size for size in (4, 3, 2, 1) if lon_cols % size == 0)

    @pl.loop(0, lon_cols // several)
    def _(i):
        block = x_ref[pl.ds(i * several, several)].astype(F32)
        block = layer_norm(block.reshape(several * lat_rows, features), gains[0:1])
        place = pl.ds(pl.multiple_of(i * (several * lat_rows), 8), several * lat_rows)
        for half in range(halves):
            normed[half, place, :] = block[:, lanes(half)]

    if slot > chunk:
        stage[...] = jnp.zeros(stage.shape, F32)

    @pl.loop(0, chunks)
    def _(ch):
        for o in range(n):
            for half in range(halves):
                for i in range(chunk):
                    row = o * rows_own + ch * chunk + i
                    taken = normed.at[half][pl.ds(row, lon_cols, stride=lat_rows), :]
                    stage.at[o % 2, half][pl.ds(i, lon_cols, stride=slot), :] = taken
                xs[o, ch, :, lanes(half)] = stage[o % 2, half].astype(BF16)
        for d in range(n - 1):
            forth(ch, d).start()
        recv[me, ch] = xs[me, ch]

    for weight, turned in ((wqkv1, wqvt1), (wqkv2, wqvt2)):
        turned[:features] = weight[:, :features].astype(F32).T.astype(BF16)
        turned[features:] = weight[:, split:].astype(F32).T.astype(BF16)

    log2e = math.log2(math.e)
    factors1 = [scales[0, h] * log2e for h in range(heads)]
    factors2 = [scales[1, h] * log2e for h in range(heads)]
    at_once = chunk if n * lon_cols <= 256 else 1

    @pl.loop(0, chunks)
    def _(ch):
        for d in range(n - 1):
            forth(ch, d).wait_recv()
        for j in range(n):
            for half in range(halves):
                arrived = recv[j, ch, :, lanes(half)].astype(F32)
                lines[half, j * tokens : (j + 1) * tokens, :] = arrived

        @pl.loop(0, chunk // at_once)
        def _(step):
            taken = []
            for k in range(at_once):
                place = pl.ds(step * at_once + k, n * lon_cols, stride=slot)
                line = [lines.at[half][place, :] for half in range(halves)]
                taken.append(jnp.concatenate(line, 1).astype(BF16))
            result = attend(
                taken, wqkv1[:, features:split], wqvt1[...], wo1[...], factors1, heads
            )
            for k in range(at_once):
                row = ch * chunk + step * at_once + k
                place = pl.ds(row, n * lon_cols, stride=rows_own)
                own = result[k * (n * lon_cols) : (k + 1) * (n * lon_cols)]
                for half in range(halves):
                    mixed.at[half][place, :] = own[:, lanes(half)]

    spare = segment - m * rows_own

    def group(t):
        return lax.rem(t + (cols_own - margin), cols_own)

    @pl.loop(0, cols_own)
    def _(t):
        c = group(t)
        for j in range(n):
            for half in range(halves):
                pieces = []
                for p in range(m):
                    start = (j * lon_cols + p * cols_own + c) * rows_own
                    if rows_own % 8 == 0:
                        start = pl.multiple_of(start, 8)
                    pieces.append(mixed[half, pl.ds(start, rows_own), :])
                if spare:
                    pieces.append(jnp.zeros((spare, LANES), F32))
                block = jnp.concatenate(pieces, 0).astype(BF16)
                obuf[j, c, :, lanes(half)] = block
        for d in range(n - 1):
            back(c, d).start()
        ret[me, c] = obuf[me, c]

    def finish_lon(c):
        for d in range(n - 1):
            back(c, d).wait_recv()
        arrived = [ret[o, c].astype(F32) for o in range(n)]
        for p in range(m):
            lon_mix = jnp.concatenate(
                [block[p * rows_own : (p + 1) * rows_own] for block in arrived], 0
            )
            first = (x_ref[p * cols_own + c].astype(F32) + lon_mix).astype(BF16).astype(F32)
            state[c, p] = first
            lsend[p, c] = layer_norm(first, gains[1:2]).astype(BF16)
        for d in range(m - 1):
            lat_forth(c, d).start()
        lrecv[mine, c] = lsend[mine, c]

    def lat_line(c):
        for d in range(m - 1):
            lat_forth(c, d).wait_recv()
        line = lrecv[:, c].reshape(m * lat_rows, features)
        result = attend(
            [line], wqkv2[:, features:split], wqvt2[...], wo2[...], factors2, heads
        )
        lout[:, c] = result.astype(BF16).reshape(m, lat_rows, features)
        for d in range(m - 1):
            lat_back(c, d).start()
        lret[mine, c] = lout[mine, c]

    def keep_rims(col, block):
        place = pl.ds(pl.multiple_of(col * 8, 8), 8)
        for half in range(halves):
            rims[0, half, place, :] = block[:8, lanes(half)]
            rims[1, half, place, :] = block[lat_rows - 8 :, lanes(half)]

    def finish_lat(c):
        for d in range(m - 1):
            lat_back(c, d).wait_recv()
        for p in range(m):
            total = (state[c, p] + lret[p, c].astype(F32)).astype(BF16)
            col = margin + p * cols_own + c
            out_ref[col] = total
            keep_rims(col, total.astype(F32))

    finish_lon(group(0))

    @pl.loop(0, cols_own)
    def _(t):
        @pl.when(t < cols_own - 1)
        def _():
            finish_lon(group(t + 1))

        lat_line(group(t))

        @pl.when(t > 0)
        def _():
            finish_lat(group(t - 1))

        if cols_own > 2 * margin:

            @pl.when(t == 2 * margin)
            def _():
                for side in range(2):
                    edge(side).start()

    finish_lat(group(cols_own - 1))
    if cols_own <= 2 * margin:
        for side in range(2):
            edge(side).start()

    for side, base in enumerate((0, margin + lon_cols)):
        edge(1 - side).wait_recv()
        for k in range(margin):
            out_ref[base + k] = erecv[side, k]
            keep_rims(base + k, erecv[side, k].astype(F32))

    ends = (mine > 0, mine < m - 1)
    for side, base in enumerate((0, 8 - margin)):
        for k in range(margin):
            for half in range(halves):
                row = rims.at[side, half][pl.ds(base + k, width, stride=8), :]
                hsend[side, k, :, lanes(half)] = row.astype(BF16)

        @pl.when(ends[side])
        def _():
            border(side).start()

    halo_ref[...] = jnp.zeros(halo_ref.shape, F32)
    for side, base in enumerate((8 - margin, 0)):

        @pl.when(ends[side])
        def _():
            border(1 - side).wait_recv()
            for k in range(margin):
                for half in range(halves):
                    row = hrecv[side, k, :, lanes(half)].astype(F32)
                    halo_ref.at[side, half][pl.ds(base + k, width, stride=8), :] = row

    for side in range(2):
        edge(side).wait_send()

        @pl.when(ends[side])
        def _():
            border(side).wait_send()

    @pl.loop(0, chunks)
    def _(ch):
        for d in range(n - 1):
            forth(ch, d).wait_send()

    @pl.loop(0, cols_own)
    def _(c):
        for d in range(n - 1):
            back(c, d).wait_send()
        for d in range(m - 1):
            lat_forth(c, d).wait_send()
            lat_back(c, d).wait_send()


def attention(fields, norm_gains, lon_qkv, lon_out, lat_qkv, lat_out, logit_scales):
    lon_cols, lat_rows, features = fields.shape
    heads = logit_scales.shape[1]
    n, m = lax.axis_size("lon"), lax.axis_size("lat")
    margin = KERNEL // 2
    width = lon_cols + 2 * margin
    rows_own, cols_own = lat_rows // n, lon_cols // m
    chunk = next(size for size in (4, 3, 2, 1) if rows_own % size == 0)
    slot = chunk
    while lon_cols * slot % 16:
        slot += 1
    tokens = lon_cols * slot
    chunks, halves = rows_own // chunk, features // LANES
    segment = -(-(m * rows_own) // 16) * 16
    vmem = pl.BlockSpec(memory_space=pltpu.VMEM)
    dma = pltpu.SemaphoreType.DMA
    groups = (m, cols_own, lat_rows, features)
    return pl.pallas_call(
        functools.partial(attention_kernel, n, m, heads, lon_cols, chunk),
        out_shape=(
            jax.ShapeDtypeStruct((width, lat_rows, features), BF16),
            jax.ShapeDtypeStruct((2, halves, width * 8, LANES), F32),
        ),
        in_specs=[vmem] * 6 + [pl.BlockSpec(memory_space=pltpu.SMEM)],
        out_specs=(vmem, vmem),
        scratch_shapes=[
            pltpu.VMEM((n, chunks, tokens, features), BF16),
            pltpu.VMEM((n, chunks, tokens, features), BF16),
            pltpu.VMEM((halves, lon_cols * lat_rows, LANES), F32),
            pltpu.VMEM((2, halves, tokens, LANES), F32),
            pltpu.VMEM((halves, n * tokens, LANES), F32),
            pltpu.VMEM((halves, n * lon_cols * rows_own, LANES), F32),
            pltpu.VMEM((n, cols_own, segment, features), BF16),
            pltpu.VMEM((n, cols_own, segment, features), BF16),
            pltpu.VMEM((cols_own, m, lat_rows, features), F32),
            pltpu.VMEM(groups, BF16),
            pltpu.VMEM(groups, BF16),
            pltpu.VMEM(groups, BF16),
            pltpu.VMEM(groups, BF16),
            pltpu.VMEM((2 * features, features), BF16),
            pltpu.VMEM((2 * features, features), BF16),
            pltpu.VMEM((2, margin, lat_rows, features), BF16),
            pltpu.VMEM((2, halves, width * 8, LANES), F32),
            pltpu.VMEM((2, margin, width, features), BF16),
            pltpu.VMEM((2, margin, width, features), BF16),
            dma((chunks, n - 1)), dma((chunks, n - 1)),
            dma((cols_own, n - 1)), dma((cols_own, n - 1)),
            dma((cols_own, m - 1)), dma((cols_own, m - 1)),
            dma((cols_own, m - 1)), dma((cols_own, m - 1)),
            dma((2,)), dma((2,)), dma((2,)), dma((2,)),
        ],
        compiler_params=pltpu.CompilerParams(
            collective_id=0, has_side_effects=True, vmem_limit_bytes=44 * 2**20
        ),
    )(fields, norm_gains, lon_qkv, lon_out, lat_qkv, lat_out, logit_scales)


def mixer_kernel(cols, wide, halo, taps, gains, w_in, w_down, out):
    first = pl.program_id(0) * cols
    rows, features = wide.shape[1:]
    hidden_len = w_down.shape[0]
    margin = KERNEL // 2
    count = cols + 2 * margin
    body = wide[pl.ds(first, count)].astype(F32)
    place = pl.ds(pl.multiple_of(first * 8, 8), count * 8)
    rims = [
        jnp.concatenate([halo[side, half, place, :] for half in range(features // LANES)], 1)
        for side in range(2)
    ]
    rims = [rim.reshape(count, 8, features) for rim in rims]
    lines = jnp.concatenate([rims[0], body, rims[1]], 1)
    smoothed = None
    for dy in range(KERNEL):
        term = None
        for dx in range(KERNEL):
            tap = taps[pl.ds(dy * KERNEL + dx, 1), :][None]
            piece = tap * lines[dx : dx + cols]
            term = piece if term is None else term + piece
        term = term[:, 8 - margin + dy : 8 - margin + dy + rows]
        smoothed = term if smoothed is None else smoothed + term
    normed = layer_norm(smoothed.reshape(cols * rows, features), gains[2:3]).astype(BF16)
    step = min(hidden_len, 256)
    update = None
    for base in range(0, hidden_len, step):
        gate = jnp.dot(normed, w_in[:, base : base + step], preferred_element_type=F32)
        up = jnp.dot(
            normed, w_in[:, hidden_len + base : hidden_len + base + step], preferred_element_type=F32
        )
        half = gate * 0.5
        hidden = (half * (1.0 + jnp.tanh(half)) * up).astype(BF16)
        share = jnp.dot(hidden, w_down[base : base + step, :], preferred_element_type=F32)
        update = share if update is None else update + share
    total = body[margin : margin + cols] + update.reshape(cols, rows, features)
    out[...] = total.astype(BF16)


def mixer(widened, halo, conv_taps, norm_gains, mlp_in, mlp_down):
    width, lat_rows, features = widened.shape
    lon_cols = width - KERNEL + 1
    cols = next(size for size in (7, 6, 5, 4, 3, 2, 1) if lon_cols % size == 0)
    vmem = pl.BlockSpec(memory_space=pltpu.VMEM)
    return pl.pallas_call(
        functools.partial(mixer_kernel, cols),
        grid=(lon_cols // cols,),
        out_shape=jax.ShapeDtypeStruct((lon_cols, lat_rows, features), BF16),
        in_specs=[vmem] * 6,
        out_specs=pl.BlockSpec((cols, lat_rows, features), lambda i: (i, 0, 0)),
        compiler_params=pltpu.CompilerParams(vmem_limit_bytes=40 * 2**20),
    )(widened, halo, conv_taps, norm_gains, mlp_in, mlp_down)


def per_device(
    fields, norm_gains, lon_qkv, lon_out, lat_qkv, lat_out, logit_scales, conv_taps, mlp_in, mlp_down
):
    columns = jnp.swapaxes(fields, 0, 1)
    widened, halo = attention(
        columns, norm_gains, lon_qkv, lon_out, lat_qkv, lat_out, logit_scales
    )
    return jnp.swapaxes(mixer(widened, halo, conv_taps, norm_gains, mlp_in, mlp_down), 0, 1)


def solution(mesh):
    in_specs = (P(("groups", "lat"), "lon", None), P(), P(), P(), P(), P(), P(), P(), P(), P())
    out_specs = P(("groups", "lat"), "lon", None)
    return jax.shard_map(
        per_device, mesh=mesh, in_specs=in_specs, out_specs=out_specs, check_vma=False
    )
```
